32 devices in a mesh: grp: 4 (over y, x), loc: 8 (over z, core).
Axes of the slice: x: 2, y: 2, z: 4, core: 2. Of those that a mesh axis runs over, the one named last changes fastest.
Arguments:
- hidden_in: bfloat16 [8, 4, 6, 3584], P('loc', 'grp'), may hold values from -6 to 6
- expert_ids: int32 [8, 4, 6, 8], P('loc', 'grp'), may hold values from 0 to 15, all different within a row; in each aligned block of 24 rows (0 to 23, 24 to 47, ..., all dimensions but the last counted through in order) at most 24 rows name the same one
- combine: bfloat16 [8, 4, 6, 8], P('loc', 'grp'), may hold values from 0.099609375 to 1
- w_gate: bfloat16 [32, 3584, 128], P(('grp', 'loc')), may hold values from -0.09375 to 0.09375
- w_up: bfloat16 [32, 3584, 128], P(('grp', 'loc')), may hold values from -0.09375 to 0.09375
- w_down: bfloat16 [32, 128, 3584], P(('grp', 'loc')), may hold values from -0.375 to 0.375
Outputs:
- layer_out: bfloat16 [8, 4, 6, 3584], P('loc', 'grp')
The draws below stay inside these ranges and needn't reach their ends.
Inputs may be any that keep to these rules, and one draw needn't show every extreme that they name: `expert_ids`: each token names 8 different experts. Among the 24 tokens of one index of loc, no expert is named more than 24 times, and in every draw some expert is named exactly 24 times there.
All inputs are finite; a program needn't handle non-finite values.
Results may differ from the reference program's by a relative error of at most 0.0066.
Values may be sent and summed in bfloat16 or wider, within the bound.
No kernel may reach another device: no remote copies, remote signals or barrier semaphores. Data moves between devices by JAX's collectives and lax.ppermute only.
A program may use at most 64 MiB of HBM per device.

```python
import math
import jax
import jax.numpy as jnp
import numpy as np
from jax import lax

D = 3584
TOP = 8
FH_DEV = 128
EXP_GRP = 4
TOK_DEV = 6
FH = 256
EXPERTS = 16
CAP = 24
BLOCKS = 32
N_GRP = 4
N_LOC = 8


def block_scale(own_key, dims, split, least, largest):
    def one(dim, shards_of):
        heights = jax.random.uniform(jax.random.fold_in(jax.random.fold_in(own_key, 6), dim), (shards_of,), jnp.float32, least / len(split), largest / len(split))
        return jnp.repeat(jnp.exp(heights), dims[dim] // shards_of).reshape((-1,) + (1,) * (len(dims) - dim - 1))

    gain = one(*split[0])
    for cut in split[1:]:
        gain = gain * one(*cut)
    return gain


def routed_block(rng, own, number, rows, count, top, limit, skew):
    order = jax.random.permutation(rng, count)
    heavy_load, common = shares(count, rows * top, limit, skew, True), shares(count, rows * top, limit, skew, False)
    places = jnp.arange(count)

    def named(lengths, rotation):
        used = int((lengths > 0).sum())
        fixed = max(1, used // 4)
        moved = fixed + (places - fixed + rotation * (used - fixed)) % max(1, count - fixed)
        return jnp.zeros((count,), jnp.int32).at[order[jnp.where(places < fixed, places, moved)]].set(jnp.asarray(lengths, jnp.int32))

    lengths = jnp.where(number % 4 == 0, named(heavy_load, number // 4), named(common, number - number // 4 - 1))
    mixed = jax.random.permutation(jax.random.fold_in(own, 3), count)
    donor, receiver = mixed[0:count // 2 * 2:2], mixed[1:count // 2 * 2:2]
    margin = jnp.minimum(lengths[donor] - 1, limit - lengths[receiver]) // 2
    margin = jnp.where((donor == order[0]) | (receiver == order[0]) | (lengths[receiver] == 0), 0, jnp.maximum(margin, 0))
    moved = jax.random.randint(jax.random.fold_in(own, 4), (count // 2,), 0, 1 << 20) % (margin + 1)
    lengths = lengths.at[donor].add(-moved).at[receiver].add(moved)
    labels = jnp.searchsorted(jnp.cumsum(lengths), jnp.arange(rows * top), side="right").astype(jnp.int32)
    table = labels.reshape(top, rows).T
    table = table[jax.random.permutation(jax.random.fold_in(own, 1), rows)]
    rotation = jax.random.randint(jax.random.fold_in(own, 2), (rows, 1), 0, top)
    return jnp.take_along_axis(table, (jnp.arange(top)[None, :] + rotation) % top, axis=1)


def shares(number_of, total, bound, lean, full):
    loads = [(1 << 20) // math.isqrt(grade ** lean) + 1 for grade in range(1, number_of + 1)]
    largest = bound if full else min(bound, max(-(-total // number_of), total * loads[0] // sum(loads)))
    least = 1 if total - largest >= number_of - 1 else 0
    given, rest = [largest] + [least] * (number_of - 1), total - largest - least * (number_of - 1)
    while rest > 0:
        candidates = [i for i in range(1, number_of) if given[i] < largest] or [i for i in range(1, number_of) if given[i] < bound]
        pool, budget = sum([loads[i] for i in candidates]), rest
        for i in candidates:
            addition = min(bound - given[i], max(1, budget * loads[i] // pool), rest)
            given[i] = given[i] + addition
            rest = rest - addition
    return np.array(given)


def scatter_about(own_key, shape, spread, bound, pieces=(), kind=jnp.bfloat16):
    values = spread * jax.random.normal(own_key, shape, jnp.float32)
    if pieces:
        values = values * block_scale(own_key, shape, pieces, -0.22, 0.18)
    return jnp.clip(values, -bound, bound).astype(kind)


def setup_inputs(seed: int = 0) -> dict:
    arg_keys = jax.random.split(jax.random.key(seed), 7)
    hidden_in = scatter_about(arg_keys[0], (N_LOC, N_GRP, TOK_DEV, D), 1.0, 6.0, ((0, 8), (1, 4)))
    expert_ids_keys = jax.random.split(jax.random.fold_in(arg_keys[1], 1), N_LOC * N_GRP * TOK_DEV // (N_GRP * TOK_DEV))
    expert_ids_turns = jax.random.permutation(jax.random.fold_in(arg_keys[1], 3), N_LOC * N_GRP * TOK_DEV // (N_GRP * TOK_DEV))
    expert_ids = jax.vmap(lambda own, number: routed_block(jax.random.fold_in(arg_keys[1], 2), own, number, N_GRP * TOK_DEV, EXPERTS, TOP, CAP, 2))(expert_ids_keys, expert_ids_turns).reshape((N_LOC, N_GRP, TOK_DEV, TOP))
    combine = jnp.clip(jnp.exp(math.log(1.0) - 2.306499 * jax.random.uniform(arg_keys[2], (N_LOC, N_GRP, TOK_DEV, TOP), jnp.float32) ** block_scale(arg_keys[2], (N_LOC, N_GRP, TOK_DEV, TOP), ((0, 8), (1, 4)), -0.2, 0.2)), 0.099609375, 1.0).astype(jnp.bfloat16)
    w_gate = scatter_about(arg_keys[3], (BLOCKS, D, FH_DEV), D ** -0.5, 0.09375, ((0, 32),))
    w_up = scatter_about(arg_keys[4], (BLOCKS, D, FH_DEV), D ** -0.5, 0.09375, ((0, 32),))
    w_down = scatter_about(arg_keys[5], (BLOCKS, FH_DEV, D), FH ** -0.5, 0.375, ((0, 32),))
    return dict(hidden_in=hidden_in, expert_ids=expert_ids, combine=combine, w_gate=w_gate, w_up=w_up, w_down=w_down)


def reference(hidden_in, expert_ids, combine, w_gate, w_up, w_down):
    token_rows = hidden_in.reshape(-1, D)
    flat_ids = expert_ids.reshape(-1)
    flat_weights = combine.reshape(-1).astype(jnp.float32)
    row_count = token_rows.shape[0]
    most = N_LOC * CAP
    slices = N_LOC // EXP_GRP

    def one_group(summed, group):
        gathered = jnp.zeros((row_count, D), jnp.float32)
        for member in range(EXP_GRP):
            expert = (group * EXP_GRP + member).astype(jnp.int32)
            is_hit = flat_ids == expert
            hit_count = jnp.sum(is_hit.astype(jnp.int32))
            positions = jnp.nonzero(is_hit, size=most, fill_value=0)[0].astype(jnp.int32)
            valid = jnp.arange(most, dtype=jnp.int32) < hit_count
            owners_row = (positions // TOP).astype(jnp.int32)
            picked = token_rows[owners_row]
            weight = jnp.where(valid, flat_weights[positions], jnp.float32(0.0))
            contrib = jnp.zeros((most, D), jnp.float32)
            for piece in range(slices):
                block = (expert * slices + piece).astype(jnp.int32)
                gate_w = lax.dynamic_index_in_dim(w_gate, block, 0, keepdims=False)
                up_w = lax.dynamic_index_in_dim(w_up, block, 0, keepdims=False)
                down_w = lax.dynamic_index_in_dim(w_down, block, 0, keepdims=False)
                gate_out = jnp.dot(picked, gate_w, preferred_element_type=jnp.float32)
                up_out = jnp.dot(picked, up_w, preferred_element_type=jnp.float32)
                hidden_block = (jax.nn.silu(gate_out) * up_out).astype(jnp.bfloat16)
                expert_part = jnp.dot(hidden_block, down_w, preferred_element_type=jnp.float32).astype(jnp.bfloat16)
                contrib = contrib + weight[:, None] * expert_part.astype(jnp.float32)
            gathered = gathered.at[owners_row].add(contrib)
        group_sum = lax.optimization_barrier(gathered.astype(jnp.bfloat16))
        return summed + group_sum.astype(jnp.float32), None

    summed, _ = lax.scan(one_group, jnp.zeros((row_count, D), jnp.float32), jnp.arange(N_GRP, dtype=jnp.int32))
    return summed.astype(jnp.bfloat16).reshape(hidden_in.shape)
```

```python
import jax
import jax.numpy as jnp
from jax import lax
from jax.sharding import PartitionSpec as P

EXP_GRP = 4
CAP = 24
LANES = 128


def packed_body(hidden_in, expert_ids, combine, w_gate, w_up, w_down):
    group_count = lax.axis_size("grp")
    loc_count = lax.axis_size("loc")
    slices = loc_count // EXP_GRP
    tok_count = hidden_in.shape[2]
    feature = hidden_in.shape[3]
    top_count = expert_ids.shape[3]
    token_rows = hidden_in.reshape(tok_count, feature)
    chosen = expert_ids.reshape(tok_count, top_count)
    weights = combine.reshape(tok_count, top_count).astype(jnp.float32)
    catalog = jnp.arange(group_count * EXP_GRP, dtype=jnp.int32)
    matches = (chosen[:, :, None] == catalog[None, None, :]).astype(jnp.float32)
    hit_table = jnp.sum(matches, axis=1)
    pick_table = jnp.einsum("tk,tke->te", weights, matches)
    hit_table = (
        hit_table.reshape(tok_count, group_count, EXP_GRP).transpose(1, 0, 2).astype(jnp.bfloat16)
    )
    pick_table = (
        pick_table.reshape(tok_count, group_count, EXP_GRP).transpose(1, 0, 2).astype(jnp.bfloat16)
    )
    arrivals_count = group_count * tok_count
    outgoing = token_rows[None, :, None, :] * hit_table[:, :, :, None]
    arrived, arr_hits, arr_picks = (
        lax.all_to_all(outgoing, "grp", split_axis=0, concat_axis=0, tiled=True),
        lax.all_to_all(hit_table, "grp", split_axis=0, concat_axis=0, tiled=True),
        lax.all_to_all(pick_table, "grp", split_axis=0, concat_axis=0, tiled=True),
    )
    arrived = arrived.reshape(arrivals_count, EXP_GRP, feature)
    flat_hits = arr_hits.reshape(arrivals_count, EXP_GRP).astype(jnp.float32)
    flat_picks = arr_picks.reshape(arrivals_count, EXP_GRP).astype(jnp.float32)
    slot_rank = jnp.cumsum(flat_hits, axis=0) - 1.0
    cell_index = jnp.arange(CAP, dtype=jnp.float32)
    selector = flat_hits.T[:, None, :] * (
        slot_rank.T[:, None, :] == cell_index[None, :, None]
    ).astype(jnp.float32)
    weighted = selector * flat_picks.T[:, None, :]
    compact_selector = selector.astype(jnp.bfloat16)
    packed = jnp.einsum(
        "jcm,mjd->jcd", compact_selector, arrived, preferred_element_type=jnp.float32
    ).astype(jnp.bfloat16)
    outbound = jnp.broadcast_to(packed[:, None, :, :], (EXP_GRP, slices, CAP, feature)).reshape(
        loc_count, CAP, feature
    )
    arrivals = lax.all_to_all(outbound, "loc", split_axis=0, concat_axis=0, tiled=True)
    item_count = arrivals.shape[1]
    flat_rows = arrivals.reshape(-1, feature)
    gate_out = jnp.dot(flat_rows, w_gate[0], preferred_element_type=jnp.float32)
    up_out = jnp.dot(flat_rows, w_up[0], preferred_element_type=jnp.float32)
    hidden_units = (jax.nn.silu(gate_out) * up_out).astype(jnp.bfloat16)
    result = jnp.dot(hidden_units, w_down[0], preferred_element_type=jnp.float32).astype(
        jnp.bfloat16
    )
    result = result.reshape(loc_count, item_count, feature)
    returned = lax.all_to_all(result, "loc", split_axis=0, concat_axis=0, tiled=True)
    slice_sum = jnp.sum(returned.reshape(EXP_GRP, slices, CAP, feature).astype(jnp.float32), axis=1)
    group_part = jnp.einsum(
        "jcm,jcd->md", weighted, slice_sum, precision=lax.Precision.HIGHEST
    ).astype(jnp.bfloat16)
    homeward = lax.all_to_all(
        group_part.reshape(group_count, tok_count, feature),
        "grp",
        split_axis=0,
        concat_axis=0,
        tiled=True,
    )
    summed = jnp.sum(homeward.astype(jnp.float32), axis=0)
    return summed.astype(jnp.bfloat16).reshape(1, 1, tok_count, feature)


def pairs(size, distance):
    return [(i, i ^ distance) for i in range(size)]


def spread(rows, axis, size, distances):
    return [rows] + [lax.ppermute(rows, axis, pairs(size, d)) for d in distances]


def fold(chunks, axis, size, distances):
    arrived = [lax.ppermute(c, axis, pairs(size, d)) for c, d in zip(chunks[1:], distances)]
    total = chunks[0].astype(jnp.float32)
    for part in arrived:
        total = total + part.astype(jnp.float32)
    return total


def dense_body(hidden_in, expert_ids, combine, w_gate, w_up, w_down):
    group_count = lax.axis_size("grp")
    loc_count = lax.axis_size("loc")
    slices = loc_count // EXP_GRP
    tok_count = hidden_in.shape[2]
    feature = hidden_in.shape[3]
    top_count = expert_ids.shape[3]
    token_rows = hidden_in.reshape(tok_count, feature)
    chosen = expert_ids.reshape(tok_count, top_count)
    weights = combine.reshape(tok_count, top_count).astype(jnp.float32)
    lanes = jnp.arange(LANES, dtype=jnp.int32)
    table = jnp.sum(
        jnp.where(chosen[:, :, None] == lanes[None, None, :], weights[:, :, None], 0.0), axis=1
    ).astype(jnp.bfloat16)
    rows = jnp.concatenate([token_rows, table], axis=1)

    member_steps = [slices * k for k in range(1, EXP_GRP)]
    group_steps = list(range(1, group_count))
    slice_steps = list(range(1, slices))
    rows = jnp.concatenate(spread(rows, "loc", loc_count, member_steps), axis=0)
    rows = jnp.concatenate(spread(rows, "grp", group_count, group_steps), axis=0)
    own_expert = lax.axis_index("grp") * EXP_GRP + lax.axis_index("loc") // slices
    pick = (lanes == own_expert).astype(jnp.float32)
    partials = []
    for block in spread(rows, "loc", loc_count, slice_steps):
        features = block[:, :feature]
        weight = jnp.sum(block[:, feature:].astype(jnp.float32) * pick[None, :], axis=1)
        gate_out = jnp.dot(features, w_gate[0], preferred_element_type=jnp.float32)
        up_out = jnp.dot(features, w_up[0], preferred_element_type=jnp.float32)
        hidden_units = (jax.nn.silu(gate_out) * up_out).astype(jnp.bfloat16)
        part = jnp.dot(hidden_units, w_down[0], preferred_element_type=jnp.float32)
        partials.append(part * weight[:, None])
    partials = partials[:1] + [p.astype(jnp.bfloat16) for p in partials[1:]]
    total = fold(partials, "loc", loc_count, slice_steps).astype(jnp.bfloat16)
    chunks = list(total.reshape(group_count, EXP_GRP * tok_count, feature))
    total = fold(chunks, "grp", group_count, group_steps).astype(jnp.bfloat16)
    chunks = list(total.reshape(EXP_GRP, tok_count, feature))
    total = fold(chunks, "loc", loc_count, member_steps).astype(jnp.bfloat16)
    return total.reshape(1, 1, tok_count, feature)


def power_of_two(count):
    return count & (count - 1) == 0


def solution(mesh):
    group_count, loc_count = mesh.shape["grp"], mesh.shape["loc"]
    placed = (
        P("loc", "grp", None, None),
        P("loc", "grp", None, None),
        P("loc", "grp", None, None),
        P(("grp", "loc"), None, None),
        P(("grp", "loc"), None, None),
        P(("grp", "loc"), None, None),
    )
    dense_fits = (
        power_of_two(group_count)
        and power_of_two(loc_count)
        and group_count * EXP_GRP <= LANES
    )

    def layer(hidden_in, *others):
        small = hidden_in.shape[1] * hidden_in.shape[2] <= CAP
        body = dense_body if dense_fits and small else packed_body
        return jax.shard_map(
            body, mesh=mesh, in_specs=placed, out_specs=P("loc", "grp", None, None), check_vma=False
        )(hidden_in, *others)

    return layer
```

```python
import functools

import jax
import jax.numpy as jnp
from jax import lax
from jax.experimental import pallas as pl
from jax.experimental.pallas import tpu as pltpu
from jax.sharding import PartitionSpec as P

EXP_GRP = 4
CAP = 24
LANES = 128


def packed_body(hidden_in, expert_ids, combine, w_gate, w_up, w_down):
    group_count = lax.axis_size("grp")
    loc_count = lax.axis_size("loc")
    slices = loc_count // EXP_GRP
    tok_count = hidden_in.shape[2]
    feature = hidden_in.shape[3]
    top_count = expert_ids.shape[3]
    token_rows = hidden_in.reshape(tok_count, feature)
    chosen = expert_ids.reshape(tok_count, top_count)
    weights = combine.reshape(tok_count, top_count).astype(jnp.float32)
    catalog = jnp.arange(group_count * EXP_GRP, dtype=jnp.int32)
    matches = (chosen[:, :, None] == catalog[None, None, :]).astype(jnp.float32)
    hit_table = jnp.sum(matches, axis=1)
    pick_table = jnp.einsum("tk,tke->te", weights, matches)
    hit_table = (
        hit_table.reshape(tok_count, group_count, EXP_GRP).transpose(1, 0, 2).astype(jnp.bfloat16)
    )
    pick_table = (
        pick_table.reshape(tok_count, group_count, EXP_GRP).transpose(1, 0, 2).astype(jnp.bfloat16)
    )
    arrivals_count = group_count * tok_count
    outgoing = token_rows[None, :, None, :] * hit_table[:, :, :, None]
    arrived, arr_hits, arr_picks = (
        lax.all_to_all(outgoing, "grp", split_axis=0, concat_axis=0, tiled=True),
        lax.all_to_all(hit_table, "grp", split_axis=0, concat_axis=0, tiled=True),
        lax.all_to_all(pick_table, "grp", split_axis=0, concat_axis=0, tiled=True),
    )
    arrived = arrived.reshape(arrivals_count, EXP_GRP, feature)
    flat_hits = arr_hits.reshape(arrivals_count, EXP_GRP).astype(jnp.float32)
    flat_picks = arr_picks.reshape(arrivals_count, EXP_GRP).astype(jnp.float32)
    slot_rank = jnp.cumsum(flat_hits, axis=0) - 1.0
    cell_index = jnp.arange(CAP, dtype=jnp.float32)
    selector = flat_hits.T[:, None, :] * (
        slot_rank.T[:, None, :] == cell_index[None, :, None]
    ).astype(jnp.float32)
    weighted = selector * flat_picks.T[:, None, :]
    compact_selector = selector.astype(jnp.bfloat16)
    packed = jnp.einsum(
        "jcm,mjd->jcd", compact_selector, arrived, preferred_element_type=jnp.float32
    ).astype(jnp.bfloat16)
    outbound = jnp.broadcast_to(packed[:, None, :, :], (EXP_GRP, slices, CAP, feature)).reshape(
        loc_count, CAP, feature
    )
    arrivals = lax.all_to_all(outbound, "loc", split_axis=0, concat_axis=0, tiled=True)
    item_count = arrivals.shape[1]
    flat_rows = arrivals.reshape(-1, feature)
    gate_out = jnp.dot(flat_rows, w_gate[0], preferred_element_type=jnp.float32)
    up_out = jnp.dot(flat_rows, w_up[0], preferred_element_type=jnp.float32)
    hidden_units = (jax.nn.silu(gate_out) * up_out).astype(jnp.bfloat16)
    result = jnp.dot(hidden_units, w_down[0], preferred_element_type=jnp.float32).astype(
        jnp.bfloat16
    )
    result = result.reshape(loc_count, item_count, feature)
    returned = lax.all_to_all(result, "loc", split_axis=0, concat_axis=0, tiled=True)
    slice_sum = jnp.sum(returned.reshape(EXP_GRP, slices, CAP, feature).astype(jnp.float32), axis=1)
    group_part = jnp.einsum(
        "jcm,jcd->md", weighted, slice_sum, precision=lax.Precision.HIGHEST
    ).astype(jnp.bfloat16)
    homeward = lax.all_to_all(
        group_part.reshape(group_count, tok_count, feature),
        "grp",
        split_axis=0,
        concat_axis=0,
        tiled=True,
    )
    summed = jnp.sum(homeward.astype(jnp.float32), axis=0)
    return summed.astype(jnp.bfloat16).reshape(1, 1, tok_count, feature)


def pairs(size, distance):
    return [(i, i ^ distance) for i in range(size)]


def spread(rows, axis, size, distances):
    return [rows] + [lax.ppermute(rows, axis, pairs(size, d)) for d in distances]


def fold(chunks, axis, size, distances):
    arrived = [lax.ppermute(c, axis, pairs(size, d)) for c, d in zip(chunks[1:], distances)]
    total = chunks[0].astype(jnp.float32)
    for part in arrived:
        total = total + part.astype(jnp.float32)
    return total


def expert_kernel(slices, rows_ref, *refs):
    gates, ups, downs, out_ref = refs[:slices], refs[slices : 2 * slices], refs[2 * slices : -1], refs[-1]
    feature = out_ref.shape[1]
    own_expert = lax.axis_index("grp") * EXP_GRP + lax.axis_index("loc") // slices
    features = rows_ref[:, :feature]
    table = rows_ref[:, feature:].astype(jnp.float32)
    lanes = lax.broadcasted_iota(jnp.int32, table.shape, 1)
    weight = jnp.sum(jnp.where(lanes == own_expert, table, 0.0), axis=1, keepdims=True)
    hidden = []
    for gate_ref, up_ref in zip(gates, ups):
        units = gate_ref.shape[1]
        both = jnp.dot(
            features,
            jnp.concatenate([gate_ref[...], up_ref[...]], axis=1),
            preferred_element_type=jnp.float32,
        )
        gate_out, up_out = both[:, :units], both[:, units:]
        hidden.append((gate_out / (1.0 + jnp.exp(-gate_out)) * up_out).astype(jnp.bfloat16))
    part = jnp.dot(
        jnp.concatenate(hidden, axis=1),
        jnp.concatenate([d[...] for d in downs], axis=0),
        preferred_element_type=jnp.float32,
    )
    out_ref[...] = (part * weight).astype(out_ref.dtype)


def run_expert(rows, gates, ups, downs):
    slices = len(gates)
    feature = downs[0].shape[1]
    count = rows.shape[0]
    weight_elements = slices * 3 * gates[0].size
    return pl.pallas_call(
        functools.partial(expert_kernel, slices),
        out_shape=jax.ShapeDtypeStruct((count, feature), jnp.bfloat16),
        in_specs=[pl.BlockSpec(memory_space=pltpu.VMEM)] * (1 + 3 * slices),
        out_specs=pl.BlockSpec(memory_space=pltpu.VMEM),
        compiler_params=pltpu.CompilerParams(vmem_limit_bytes=32 * 1024 * 1024),
        cost_estimate=pl.CostEstimate(
            flops=2 * count * weight_elements,
            bytes_accessed=2 * weight_elements,
            transcendentals=count * slices * gates[0].shape[1],
        ),
    )(rows, *gates, *ups, *downs)


def dense_body(hidden_in, expert_ids, combine, w_gate, w_up, w_down):
    group_count = lax.axis_size("grp")
    loc_count = lax.axis_size("loc")
    slices = loc_count // EXP_GRP
    tok_count = hidden_in.shape[2]
    feature = hidden_in.shape[3]
    top_count = expert_ids.shape[3]
    token_rows = hidden_in.reshape(tok_count, feature)
    chosen = expert_ids.reshape(tok_count, top_count)
    weights = combine.reshape(tok_count, top_count).astype(jnp.float32)
    lanes = jnp.arange(LANES, dtype=jnp.int32)
    table = jnp.sum(
        jnp.where(chosen[:, :, None] == lanes[None, None, :], weights[:, :, None], 0.0), axis=1
    ).astype(jnp.bfloat16)
    rows = jnp.concatenate([token_rows, table], axis=1)

    member_steps = [slices * k for k in range(1, EXP_GRP)]
    group_steps = list(range(1, group_count))
    slice_steps = list(range(1, slices))
    gates, ups, downs = (
        spread(w[0], "loc", loc_count, slice_steps) for w in (w_gate, w_up, w_down)
    )
    rows = jnp.concatenate(spread(rows, "loc", loc_count, member_steps), axis=0)
    partials = [
        run_expert(block, gates, ups, downs)
        for block in spread(rows, "grp", group_count, group_steps)
    ]
    total = fold(partials, "grp", group_count, group_steps).astype(jnp.bfloat16)
    chunks = list(total.reshape(EXP_GRP, tok_count, feature))
    total = fold(chunks, "loc", loc_count, member_steps).astype(jnp.bfloat16)
    return total.reshape(1, 1, tok_count, feature)


def power_of_two(count):
    return count & (count - 1) == 0


def solution(mesh):
    group_count, loc_count = mesh.shape["grp"], mesh.shape["loc"]
    placed = (
        P("loc", "grp", None, None),
        P("loc", "grp", None, None),
        P("loc", "grp", None, None),
        P(("grp", "loc"), None, None),
        P(("grp", "loc"), None, None),
        P(("grp", "loc"), None, None),
    )
    dense_fits = (
        power_of_two(group_count)
        and power_of_two(loc_count)
        and group_count * EXP_GRP <= LANES
    )

    def layer(hidden_in, *others):
        small = hidden_in.shape[1] * hidden_in.shape[2] <= CAP
        body = dense_body if dense_fits and small else packed_body
        return jax.shard_map(
            body, mesh=mesh, in_specs=placed, out_specs=P("loc", "grp", None, None), check_vma=False
        )(hidden_in, *others)

    return layer
```

```python
import functools

import jax
import jax.numpy as jnp
from jax import lax
from jax.experimental import pallas as pl
from jax.experimental.pallas import tpu as pltpu
from jax.sharding import PartitionSpec as P

EXP_GRP = 4
CAP = 24
LANES = 128
SUBLANES = 8


def packed_body(hidden_in, expert_ids, combine, w_gate, w_up, w_down):
    group_count = lax.axis_size("grp")
    loc_count = lax.axis_size("loc")
    slices = loc_count // EXP_GRP
    tok_count = hidden_in.shape[2]
    feature = hidden_in.shape[3]
    top_count = expert_ids.shape[3]
    token_rows = hidden_in.reshape(tok_count, feature)
    chosen = expert_ids.reshape(tok_count, top_count)
    weights = combine.reshape(tok_count, top_count).astype(jnp.float32)
    catalog = jnp.arange(group_count * EXP_GRP, dtype=jnp.int32)
    matches = (chosen[:, :, None] == catalog[None, None, :]).astype(jnp.float32)
    hit_table = jnp.sum(matches, axis=1)
    pick_table = jnp.einsum("tk,tke->te", weights, matches)
    hit_table = (
        hit_table.reshape(tok_count, group_count, EXP_GRP).transpose(1, 0, 2).astype(jnp.bfloat16)
    )
    pick_table = (
        pick_table.reshape(tok_count, group_count, EXP_GRP).transpose(1, 0, 2).astype(jnp.bfloat16)
    )
    arrivals_count = group_count * tok_count
    outgoing = token_rows[None, :, None, :] * hit_table[:, :, :, None]
    arrived, arr_hits, arr_picks = (
        lax.all_to_all(outgoing, "grp", split_axis=0, concat_axis=0, tiled=True),
        lax.all_to_all(hit_table, "grp", split_axis=0, concat_axis=0, tiled=True),
        lax.all_to_all(pick_table, "grp", split_axis=0, concat_axis=0, tiled=True),
    )
    arrived = arrived.reshape(arrivals_count, EXP_GRP, feature)
    flat_hits = arr_hits.reshape(arrivals_count, EXP_GRP).astype(jnp.float32)
    flat_picks = arr_picks.reshape(arrivals_count, EXP_GRP).astype(jnp.float32)
    slot_rank = jnp.cumsum(flat_hits, axis=0) - 1.0
    cell_index = jnp.arange(CAP, dtype=jnp.float32)
    selector = flat_hits.T[:, None, :] * (
        slot_rank.T[:, None, :] == cell_index[None, :, None]
    ).astype(jnp.float32)
    weighted = selector * flat_picks.T[:, None, :]
    compact_selector = selector.astype(jnp.bfloat16)
    packed = jnp.einsum(
        "jcm,mjd->jcd", compact_selector, arrived, preferred_element_type=jnp.float32
    ).astype(jnp.bfloat16)
    outbound = jnp.broadcast_to(packed[:, None, :, :], (EXP_GRP, slices, CAP, feature)).reshape(
        loc_count, CAP, feature
    )
    arrivals = lax.all_to_all(outbound, "loc", split_axis=0, concat_axis=0, tiled=True)
    item_count = arrivals.shape[1]
    flat_rows = arrivals.reshape(-1, feature)
    gate_out = jnp.dot(flat_rows, w_gate[0], preferred_element_type=jnp.float32)
    up_out = jnp.dot(flat_rows, w_up[0], preferred_element_type=jnp.float32)
    hidden_units = (jax.nn.silu(gate_out) * up_out).astype(jnp.bfloat16)
    result = jnp.dot(hidden_units, w_down[0], preferred_element_type=jnp.float32).astype(
        jnp.bfloat16
    )
    result = result.reshape(loc_count, item_count, feature)
    returned = lax.all_to_all(result, "loc", split_axis=0, concat_axis=0, tiled=True)
    slice_sum = jnp.sum(returned.reshape(EXP_GRP, slices, CAP, feature).astype(jnp.float32), axis=1)
    group_part = jnp.einsum(
        "jcm,jcd->md", weighted, slice_sum, precision=lax.Precision.HIGHEST
    ).astype(jnp.bfloat16)
    homeward = lax.all_to_all(
        group_part.reshape(group_count, tok_count, feature),
        "grp",
        split_axis=0,
        concat_axis=0,
        tiled=True,
    )
    summed = jnp.sum(homeward.astype(jnp.float32), axis=0)
    return summed.astype(jnp.bfloat16).reshape(1, 1, tok_count, feature)


def pairs(size, distance):
    return [(i, i ^ distance) for i in range(size)]


def swap(rows, axis, distance):
    return lax.ppermute(rows, axis, pairs(lax.axis_size(axis), distance))


def tails_per_row(tok_count):
    return tok_count // (SUBLANES - tok_count)


def tail_width(tok_count, feature):
    return feature // (tails_per_row(tok_count) + 1)


def can_pack(tok_count, feature):
    spare = SUBLANES - tok_count
    if spare <= 0 or tok_count % spare:
        return False
    return feature % (LANES * (tails_per_row(tok_count) + 1)) == 0


def tail_places(tok_count, feature):
    per_row, width = tails_per_row(tok_count), tail_width(tok_count, feature)
    for t in range(tok_count):
        yield t, tok_count + t // per_row, (t % per_row) * width, width


def pack_rows(source, first, tok_count, feature, target):
    body = feature - tail_width(tok_count, feature)
    target[:tok_count, :body] = source[first : first + tok_count, :body]
    for t, row, lane, width in tail_places(tok_count, feature):
        target[row : row + 1, lane : lane + width] = source[first + t : first + t + 1, body:feature]


def unpack_rows(source, target, first, tok_count, feature):
    body = feature - tail_width(tok_count, feature)
    target[first : first + tok_count, :body] = source[:tok_count, :body]
    for t, row, lane, width in tail_places(tok_count, feature):
        target[first + t : first + t + 1, body:feature] = source[row : row + 1, lane : lane + width]


VMEM = pl.BlockSpec(memory_space=pltpu.VMEM)
HBM = pl.BlockSpec(memory_space=pltpu.HBM)


def in_hbm(array):
    return pltpu.with_memory_space_constraint(array, pltpu.HBM)


def call(kernel, outs, args, scratch=(), specs=None, flops=0, traffic=0):
    return pl.pallas_call(
        kernel,
        out_shape=outs,
        in_specs=specs or [VMEM] * len(args),
        out_specs=jax.tree.map(lambda _: VMEM, outs),
        scratch_shapes=list(scratch),
        compiler_params=pltpu.CompilerParams(vmem_limit_bytes=24 * 1024 * 1024),
        cost_estimate=pl.CostEstimate(flops=flops, bytes_accessed=traffic, transcendentals=0),
    )(*args)


def prepare_kernel(rows_hbm, ids_hbm, combine_hbm, out_ref, rows, ids, picks, wide, packed, sems):
    copies = [
        pltpu.make_async_copy(source, target, sems.at[i])
        for i, (source, target) in enumerate(
            ((rows_hbm, rows), (ids_hbm, ids), (combine_hbm, picks))
        )
    ]
    for c in copies:
        c.start()
    for c in copies:
        c.wait()
    tok_count, feature = rows.shape
    body = feature - tail_width(tok_count, feature)
    wide[...] = rows[...].astype(jnp.float32)
    packed[:, body:] = jnp.zeros((SUBLANES, LANES), jnp.float32)
    pack_rows(wide, 0, tok_count, feature, packed)
    weights = picks[...].astype(jnp.float32)
    lanes = lax.broadcasted_iota(jnp.int32, (1, LANES), 1)
    for t in range(tok_count):
        chosen = ids[t]
        row = jnp.zeros((1, LANES), jnp.float32)
        for k in range(chosen.shape[1]):
            row = row + jnp.where(lanes == chosen[:, k : k + 1], weights[t : t + 1, k : k + 1], 0.0)
        packed[t : t + 1, body:] = row
    out_ref[...] = packed[...].astype(jnp.bfloat16)


def join_kernel(tok_count, feature, *refs):
    pieces, out_ref, narrow, wide = refs[:-3], refs[-3], refs[-2], refs[-1]
    body = feature - tail_width(tok_count, feature)
    for i, piece in enumerate(pieces):
        narrow[...] = piece[...].astype(jnp.float32)
        unpack_rows(narrow, wide, i * tok_count, tok_count, feature)
        wide[i * tok_count : (i + 1) * tok_count, feature:] = narrow[:tok_count, body:]
    out_ref[...] = wide[...].astype(jnp.bfloat16)


def fetch_kernel(*refs):
    count = (len(refs) - 1) // 2
    sems = refs[-1]
    copies = [
        pltpu.make_async_copy(refs[i], refs[count + i], sems.at[i]) for i in range(count)
    ]
    for c in copies:
        c.start()
    for c in copies:
        c.wait()


def expert_kernel(slices, rows_ref, *refs):
    gates, ups, downs, out_ref = refs[:slices], refs[slices : 2 * slices], refs[2 * slices : -1], refs[-1]
    feature = out_ref.shape[1]
    own_expert = lax.axis_index("grp") * EXP_GRP + lax.axis_index("loc") // slices
    features = rows_ref[:, :feature]
    table = rows_ref[:, feature:].astype(jnp.float32)
    lanes = lax.broadcasted_iota(jnp.int32, table.shape, 1)
    weight = jnp.sum(jnp.where(lanes == own_expert, table, 0.0), axis=1, keepdims=True)
    hidden = []
    for gate_ref, up_ref in zip(gates, ups):
        units = gate_ref.shape[1]
        both = jnp.dot(
            features,
            jnp.concatenate([gate_ref[...], up_ref[...]], axis=1),
            preferred_element_type=jnp.float32,
        )
        gate_out, up_out = both[:, :units], both[:, units:]
        hidden.append((gate_out / (1.0 + jnp.exp(-gate_out)) * up_out).astype(jnp.bfloat16))
    part = jnp.dot(
        jnp.concatenate(hidden, axis=1),
        jnp.concatenate([d[...] for d in downs], axis=0),
        preferred_element_type=jnp.float32,
    )
    out_ref[...] = (part * weight).astype(out_ref.dtype)


def combine_kernel(tok_count, parts, *refs):
    pieces, outs, wide, packed = refs[:parts], refs[parts:-2], refs[-2], refs[-1]
    total = pieces[0][...].astype(jnp.float32)
    for piece in pieces[1:]:
        total = total + piece[...].astype(jnp.float32)
    wide[...] = total
    feature = wide.shape[1]
    for i, out_ref in enumerate(outs):
        pack_rows(wide, i * tok_count, tok_count, feature, packed)
        out_ref[...] = packed[...].astype(out_ref.dtype)


def finish_kernel(*refs):
    pieces, out_ref, packed, wide = refs[:-3], refs[-3], refs[-2], refs[-1]
    total = pieces[0][...].astype(jnp.float32)
    for piece in pieces[1:]:
        total = total + piece[...].astype(jnp.float32)
    packed[...] = total
    unpack_rows(packed, wide, 0, *wide.shape)
    out_ref[...] = wide[...].astype(out_ref.dtype)


def dense_body(hidden_in, expert_ids, combine, w_gate, w_up, w_down):
    group_count = lax.axis_size("grp")
    slices = lax.axis_size("loc") // EXP_GRP
    tok_count = hidden_in.shape[2]
    feature = hidden_in.shape[3]
    top_count = expert_ids.shape[3]
    gathered = EXP_GRP * tok_count
    body = feature - tail_width(tok_count, feature)
    bf16, f32 = jnp.bfloat16, jnp.float32
    scratch = pltpu.VMEM

    blocks = (w_gate[0], w_up[0], w_down[0])
    own = call(
        prepare_kernel,
        jax.ShapeDtypeStruct((SUBLANES, body + LANES), bf16),
        (
            in_hbm(hidden_in.reshape(tok_count, feature)),
            in_hbm(expert_ids.reshape(tok_count, 1, top_count)),
            in_hbm(combine.reshape(tok_count, top_count)),
        ),
        [
            scratch((tok_count, feature), bf16),
            scratch((tok_count, 1, top_count), jnp.int32),
            scratch((tok_count, top_count), bf16),
            scratch((tok_count, feature), f32),
            scratch((SUBLANES, body + LANES), f32),
            pltpu.SemaphoreType.DMA((3,)),
        ],
        [HBM] * 3,
    )
    *blocks, own = lax.optimization_barrier((*blocks, own))
    pieces = [own] + [swap(own, "loc", slices * k) for k in range(1, EXP_GRP)]
    others = [[swap(w, "loc", k) for w in blocks] for k in range(1, slices)]
    size = sum(w.size for w in blocks)
    kept = call(
        fetch_kernel,
        [jax.ShapeDtypeStruct(w.shape, w.dtype) for w in blocks],
        [in_hbm(w) for w in blocks],
        [pltpu.SemaphoreType.DMA((len(blocks),))],
        [HBM] * len(blocks),
        traffic=2 * size,
    )
    pieces, others, kept = lax.optimization_barrier((pieces, others, kept))
    gates, ups, downs = zip(kept, *others)
    rows = call(
        functools.partial(join_kernel, tok_count, feature),
        jax.ShapeDtypeStruct((gathered, feature + LANES), bf16),
        pieces,
        [scratch((SUBLANES, body + LANES), f32), scratch((gathered, feature + LANES), f32)],
    )

    def run_expert(block):
        return call(
            functools.partial(expert_kernel, slices),
            jax.ShapeDtypeStruct((gathered, feature), bf16),
            (block, *gates, *ups, *downs),
            flops=2 * gathered * size * slices,
            traffic=2 * size * slices,
        )

    arrived = [swap(rows, "grp", k) for k in range(1, group_count)]
    parts = [run_expert(rows)]
    returned = []
    for k, block in enumerate(arrived, 1):
        parts.append(run_expert(block))
        returned.append(swap(parts[-1], "grp", k))
    packed = jax.ShapeDtypeStruct((SUBLANES, body), bf16)
    sums = call(
        functools.partial(combine_kernel, tok_count, group_count),
        [jax.ShapeDtypeStruct(packed.shape, f32)] + [packed] * (EXP_GRP - 1),
        (parts[0], *returned),
        [scratch((gathered, feature), f32), scratch(packed.shape, f32)],
    )
    homeward = [swap(s, "loc", slices * k) for k, s in enumerate(sums[1:], 1)]
    total = call(
        finish_kernel,
        jax.ShapeDtypeStruct((tok_count, feature), bf16),
        (sums[0], *homeward),
        [scratch(packed.shape, f32), scratch((tok_count, feature), f32)],
    )
    return total.reshape(1, 1, tok_count, feature)


def power_of_two(count):
    return count & (count - 1) == 0


def solution(mesh):
    group_count, loc_count = mesh.shape["grp"], mesh.shape["loc"]
    placed = (
        P("loc", "grp", None, None),
        P("loc", "grp", None, None),
        P("loc", "grp", None, None),
        P(("grp", "loc"), None, None),
        P(("grp", "loc"), None, None),
        P(("grp", "loc"), None, None),
    )
    dense_fits = (
        power_of_two(group_count)
        and power_of_two(loc_count)
        and group_count * EXP_GRP <= LANES
    )

    def layer(hidden_in, *others):
        tokens = hidden_in.shape[1] * hidden_in.shape[2]
        small = tokens <= CAP and can_pack(*hidden_in.shape[2:])
        body = dense_body if dense_fits and small else packed_body
        return jax.shard_map(
            body, mesh=mesh, in_specs=placed, out_specs=P("loc", "grp", None, None), check_vma=False
        )(hidden_in, *others)

    return layer
```

```python
import functools

import jax
import jax.numpy as jnp
from jax import lax
from jax.experimental import pallas as pl
from jax.experimental.pallas import tpu as pltpu
from jax.sharding import PartitionSpec as P

EXP_GRP = 4
CAP = 24
LANES = 128
SUBLANES = 8


def packed_body(hidden_in, expert_ids, combine, w_gate, w_up, w_down):
    group_count = lax.axis_size("grp")
    loc_count = lax.axis_size("loc")
    slices = loc_count // EXP_GRP
    tok_count = hidden_in.shape[2]
    feature = hidden_in.shape[3]
    top_count = expert_ids.shape[3]
    token_rows = hidden_in.reshape(tok_count, feature)
    chosen = expert_ids.reshape(tok_count, top_count)
    weights = combine.reshape(tok_count, top_count).astype(jnp.float32)
    catalog = jnp.arange(group_count * EXP_GRP, dtype=jnp.int32)
    matches = (chosen[:, :, None] == catalog[None, None, :]).astype(jnp.float32)
    hit_table = jnp.sum(matches, axis=1)
    pick_table = jnp.einsum("tk,tke->te", weights, matches)
    hit_table = (
        hit_table.reshape(tok_count, group_count, EXP_GRP).transpose(1, 0, 2).astype(jnp.bfloat16)
    )
    pick_table = (
        pick_table.reshape(tok_count, group_count, EXP_GRP).transpose(1, 0, 2).astype(jnp.bfloat16)
    )
    arrivals_count = group_count * tok_count
    outgoing = token_rows[None, :, None, :] * hit_table[:, :, :, None]
    arrived, arr_hits, arr_picks = (
        lax.all_to_all(outgoing, "grp", split_axis=0, concat_axis=0, tiled=True),
        lax.all_to_all(hit_table, "grp", split_axis=0, concat_axis=0, tiled=True),
        lax.all_to_all(pick_table, "grp", split_axis=0, concat_axis=0, tiled=True),
    )
    arrived = arrived.reshape(arrivals_count, EXP_GRP, feature)
    flat_hits = arr_hits.reshape(arrivals_count, EXP_GRP).astype(jnp.float32)
    flat_picks = arr_picks.reshape(arrivals_count, EXP_GRP).astype(jnp.float32)
    slot_rank = jnp.cumsum(flat_hits, axis=0) - 1.0
    cell_index = jnp.arange(CAP, dtype=jnp.float32)
    selector = flat_hits.T[:, None, :] * (
        slot_rank.T[:, None, :] == cell_index[None, :, None]
    ).astype(jnp.float32)
    weighted = selector * flat_picks.T[:, None, :]
    compact_selector = selector.astype(jnp.bfloat16)
    packed = jnp.einsum(
        "jcm,mjd->jcd", compact_selector, arrived, preferred_element_type=jnp.float32
    ).astype(jnp.bfloat16)
    outbound = jnp.broadcast_to(packed[:, None, :, :], (EXP_GRP, slices, CAP, feature)).reshape(
        loc_count, CAP, feature
    )
    arrivals = lax.all_to_all(outbound, "loc", split_axis=0, concat_axis=0, tiled=True)
    item_count = arrivals.shape[1]
    flat_rows = arrivals.reshape(-1, feature)
    gate_out = jnp.dot(flat_rows, w_gate[0], preferred_element_type=jnp.float32)
    up_out = jnp.dot(flat_rows, w_up[0], preferred_element_type=jnp.float32)
    hidden_units = (jax.nn.silu(gate_out) * up_out).astype(jnp.bfloat16)
    result = jnp.dot(hidden_units, w_down[0], preferred_element_type=jnp.float32).astype(
        jnp.bfloat16
    )
    result = result.reshape(loc_count, item_count, feature)
    returned = lax.all_to_all(result, "loc", split_axis=0, concat_axis=0, tiled=True)
    slice_sum = jnp.sum(returned.reshape(EXP_GRP, slices, CAP, feature).astype(jnp.float32), axis=1)
    group_part = jnp.einsum(
        "jcm,jcd->md", weighted, slice_sum, precision=lax.Precision.HIGHEST
    ).astype(jnp.bfloat16)
    homeward = lax.all_to_all(
        group_part.reshape(group_count, tok_count, feature),
        "grp",
        split_axis=0,
        concat_axis=0,
        tiled=True,
    )
    summed = jnp.sum(homeward.astype(jnp.float32), axis=0)
    return summed.astype(jnp.bfloat16).reshape(1, 1, tok_count, feature)


def pairs(size, distance):
    return [(i, i ^ distance) for i in range(size)]


def swap(rows, axis, distance):
    return lax.ppermute(rows, axis, pairs(lax.axis_size(axis), distance))


def slide(rows, distance):
    count = lax.axis_size("loc")
    return lax.ppermute(rows, "loc", [(i, (i + distance) % count) for i in range(count)])


def turn(rows, steps):
    loc_count = lax.axis_size("loc")
    moves = [
        (g * loc_count + l, (g ^ steps[l % len(steps)]) * loc_count + l)
        for g in range(lax.axis_size("grp"))
        for l in range(loc_count)
    ]
    return lax.ppermute(rows, ("grp", "loc"), moves)


def tails_per_row(tok_count):
    return tok_count // (SUBLANES - tok_count)


def tail_width(tok_count, feature):
    return feature // (tails_per_row(tok_count) + 1)


def can_pack(tok_count, feature):
    spare = SUBLANES - tok_count
    if spare <= 0 or tok_count % spare:
        return False
    return feature % (LANES * (tails_per_row(tok_count) + 1)) == 0


def tail_places(tok_count, feature):
    per_row, width = tails_per_row(tok_count), tail_width(tok_count, feature)
    for t in range(tok_count):
        yield t, tok_count + t // per_row, (t % per_row) * width, width


def pack_rows(source, first, tok_count, feature, target):
    body = feature - tail_width(tok_count, feature)
    target[:tok_count, :body] = source[first : first + tok_count, :body]
    for t, row, lane, width in tail_places(tok_count, feature):
        target[row : row + 1, lane : lane + width] = source[first + t : first + t + 1, body:feature]


def unpack_rows(source, target, first, tok_count, feature):
    body = feature - tail_width(tok_count, feature)
    target[first : first + tok_count, :body] = source[:tok_count, :body]
    for t, row, lane, width in tail_places(tok_count, feature):
        target[first + t : first + t + 1, body:feature] = source[row : row + 1, lane : lane + width]


VMEM = pl.BlockSpec(memory_space=pltpu.VMEM)
HBM = pl.BlockSpec(memory_space=pltpu.HBM)


def in_hbm(array):
    return pltpu.with_memory_space_constraint(array, pltpu.HBM)


def call(kernel, outs, args, scratch=(), specs=None, flops=0, traffic=0):
    return pl.pallas_call(
        kernel,
        out_shape=outs,
        in_specs=specs or [VMEM] * len(args),
        out_specs=jax.tree.map(lambda _: VMEM, outs),
        scratch_shapes=list(scratch),
        compiler_params=pltpu.CompilerParams(vmem_limit_bytes=24 * 1024 * 1024),
        cost_estimate=pl.CostEstimate(flops=flops, bytes_accessed=traffic, transcendentals=0),
    )(*args)


def prepare_kernel(rows_hbm, ids_hbm, combine_hbm, out_ref, rows, ids, picks, wide, packed, sems):
    copies = [
        pltpu.make_async_copy(source, target, sems.at[i])
        for i, (source, target) in enumerate(
            ((rows_hbm, rows), (ids_hbm, ids), (combine_hbm, picks))
        )
    ]
    for c in copies:
        c.start()
    for c in copies:
        c.wait()
    tok_count, feature = rows.shape
    body = feature - tail_width(tok_count, feature)
    wide[...] = rows[...].astype(jnp.float32)
    packed[:, body:] = jnp.zeros((SUBLANES, LANES), jnp.float32)
    pack_rows(wide, 0, tok_count, feature, packed)
    weights = picks[...].astype(jnp.float32)
    lanes = lax.broadcasted_iota(jnp.int32, (1, LANES), 1)
    for t in range(tok_count):
        chosen = ids[t]
        row = jnp.zeros((1, LANES), jnp.float32)
        for k in range(chosen.shape[1]):
            row = row + jnp.where(lanes == chosen[:, k : k + 1], weights[t : t + 1, k : k + 1], 0.0)
        packed[t : t + 1, body:] = row
    out_ref[...] = packed[...].astype(jnp.bfloat16)


def join_kernel(*refs):
    pieces, out_ref = refs[:-1], refs[-1]
    out_ref[...] = jnp.concatenate([piece[...] for piece in pieces], axis=0)


def fetch_kernel(gate_hbm, up_hbm, down_hbm, out_ref, sems):
    feature, units = gate_hbm.shape
    copies = [
        (gate_hbm, out_ref.at[:feature]),
        (up_hbm, out_ref.at[feature : 2 * feature]),
    ]
    for i in range(feature // LANES):
        lowest = 2 * feature + i * units
        copies.append(
            (down_hbm.at[:, i * LANES : (i + 1) * LANES], out_ref.at[lowest : lowest + units])
        )
    copies = [
        pltpu.make_async_copy(source, target, sems.at[i])
        for i, (source, target) in enumerate(copies)
    ]
    for c in copies:
        c.start()
    for c in copies:
        c.wait()


def expert_kernel(tok_count, slices, rows_ref, *refs):
    weights, (out_ref, narrow, wide) = refs[:slices], refs[slices:]
    units = LANES
    feature = wide.shape[1] - LANES
    body = feature - tail_width(tok_count, feature)
    own_expert = lax.axis_index("grp") * EXP_GRP + lax.axis_index("loc") // slices
    for i in range(EXP_GRP):
        narrow[...] = rows_ref[i * SUBLANES : (i + 1) * SUBLANES, :].astype(jnp.float32)
        unpack_rows(narrow, wide, i * tok_count, tok_count, feature)
        wide[i * tok_count : (i + 1) * tok_count, feature:] = narrow[:tok_count, body:]
    features = wide[:, :feature].astype(jnp.bfloat16)
    table = wide[:, feature:]
    lanes = lax.broadcasted_iota(jnp.int32, table.shape, 1)
    weight = jnp.sum(jnp.where(lanes == own_expert, table, 0.0), axis=1, keepdims=True)
    hidden, downs = [], []
    for w in weights:
        both = jnp.dot(
            features,
            jnp.concatenate([w[:feature], w[feature : 2 * feature]], axis=1),
            preferred_element_type=jnp.float32,
        )
        gate_out, up_out = both[:, :units], both[:, units:]
        hidden.append((gate_out / (1.0 + jnp.exp(-gate_out)) * up_out).astype(jnp.bfloat16))
        blocks = [
            w[2 * feature + i * units : 2 * feature + (i + 1) * units]
            for i in range(feature // LANES)
        ]
        downs.append(jnp.concatenate(blocks, axis=1))
    part = jnp.dot(
        jnp.concatenate(hidden, axis=1),
        jnp.concatenate(downs, axis=0),
        preferred_element_type=jnp.float32,
    )
    wide[:, :feature] = part * weight
    for i in range(EXP_GRP):
        pack_rows(wide, i * tok_count, tok_count, feature, narrow)
        out_ref[i * SUBLANES : (i + 1) * SUBLANES, :] = narrow[:, :body].astype(out_ref.dtype)


def combine_kernel(*refs):
    pieces, outs = refs[:EXP_GRP], refs[EXP_GRP:]
    total = pieces[0][...].astype(jnp.float32)
    for piece in pieces[1:]:
        total = total + piece[...].astype(jnp.float32)
    for i, out_ref in enumerate(outs):
        out_ref[...] = total[i * SUBLANES : (i + 1) * SUBLANES].astype(out_ref.dtype)


def finish_kernel(*refs):
    pieces, out_ref, packed, wide = refs[:-3], refs[-3], refs[-2], refs[-1]
    total = pieces[0][...].astype(jnp.float32)
    for piece in pieces[1:]:
        total = total + piece[...].astype(jnp.float32)
    packed[...] = total
    unpack_rows(packed, wide, 0, *wide.shape)
    out_ref[...] = wide[...].astype(out_ref.dtype)


def dense_body(hidden_in, expert_ids, combine, w_gate, w_up, w_down):
    slices = lax.axis_size("loc") // EXP_GRP
    tok_count = hidden_in.shape[2]
    feature = hidden_in.shape[3]
    top_count = expert_ids.shape[3]
    gathered = EXP_GRP * tok_count
    body = feature - tail_width(tok_count, feature)
    bf16, f32 = jnp.bfloat16, jnp.float32
    scratch = pltpu.VMEM

    blocks = (w_gate[0], w_up[0], w_down[0])
    own = call(
        prepare_kernel,
        jax.ShapeDtypeStruct((SUBLANES, body + LANES), bf16),
        (
            in_hbm(hidden_in.reshape(tok_count, feature)),
            in_hbm(expert_ids.reshape(tok_count, 1, top_count)),
            in_hbm(combine.reshape(tok_count, top_count)),
        ),
        [
            scratch((tok_count, feature), bf16),
            scratch((tok_count, 1, top_count), jnp.int32),
            scratch((tok_count, top_count), bf16),
            scratch((tok_count, feature), f32),
            scratch((SUBLANES, body + LANES), f32),
            pltpu.SemaphoreType.DMA((3,)),
        ],
        [HBM] * 3,
    )
    steps = range(1, EXP_GRP)
    pieces = [own] + [slide(own, slices * k) for k in steps]
    *blocks, pieces[0] = lax.optimization_barrier((*blocks, pieces[0]))
    size = sum(w.size for w in blocks)
    kept = call(
        fetch_kernel,
        jax.ShapeDtypeStruct((3 * feature, LANES), bf16),
        [in_hbm(w) for w in blocks],
        [pltpu.SemaphoreType.DMA((2 + feature // LANES,))],
        [HBM] * 3,
        traffic=2 * size,
    )
    kept, pieces = lax.optimization_barrier((kept, pieces))
    weights = [kept] + [swap(kept, "loc", k) for k in range(1, slices)]

    def run_expert(rows, dtype):
        return call(
            functools.partial(expert_kernel, tok_count, slices),
            jax.ShapeDtypeStruct((EXP_GRP * SUBLANES, body), dtype),
            (rows, *weights),
            [scratch((SUBLANES, body + LANES), f32), scratch((gathered, feature + LANES), f32)],
            flops=2 * gathered * size * slices,
            traffic=2 * size * slices,
        )

    rows = call(
        join_kernel, jax.ShapeDtypeStruct((EXP_GRP * SUBLANES, body + LANES), bf16), pieces
    )
    first, second = [1 + i % 2 for i in range(slices)], [2 - i % 2 for i in range(slices)]
    beside, above = turn(rows, first), turn(rows, second)
    across = turn(beside, second)
    returned = (
        turn(run_expert(beside, bf16), first),
        turn(run_expert(above, bf16), second),
        swap(run_expert(across, bf16), "grp", 3),
    )
    packed = (SUBLANES, body)
    sums = call(
        combine_kernel,
        [jax.ShapeDtypeStruct(packed, f32)] + [jax.ShapeDtypeStruct(packed, bf16)] * len(steps),
        (run_expert(rows, f32), *returned),
    )
    homeward = [slide(sums[k], -slices * k) for k in steps]
    total = call(
        finish_kernel,
        jax.ShapeDtypeStruct((tok_count, feature), bf16),
        (sums[0], *homeward),
        [scratch(packed, f32), scratch((tok_count, feature), f32)],
    )
    return total.reshape(1, 1, tok_count, feature)


def power_of_two(count):
    return count & (count - 1) == 0


def solution(mesh):
    group_count, loc_count = mesh.shape["grp"], mesh.shape["loc"]
    placed = (
        P("loc", "grp", None, None),
        P("loc", "grp", None, None),
        P("loc", "grp", None, None),
        P(("grp", "loc"), None, None),
        P(("grp", "loc"), None, None),
        P(("grp", "loc"), None, None),
    )
    dense_fits = group_count == EXP_GRP == 4 and power_of_two(loc_count)

    def layer(hidden_in, *others):
        tokens = hidden_in.shape[1] * hidden_in.shape[2]
        units = others[2].shape[2]
        small = tokens <= CAP and units == LANES and can_pack(*hidden_in.shape[2:])
        body = dense_body if dense_fits and small else packed_body
        return jax.shard_map(
            body, mesh=mesh, in_specs=placed, out_specs=P("loc", "grp", None, None), check_vma=False
        )(hidden_in, *others)

    return layer
```

```python
import functools

import jax
import jax.numpy as jnp
from jax import lax
from jax.experimental import pallas as pl
from jax.experimental.pallas import tpu as pltpu
from jax.sharding import PartitionSpec as P

EXP_GRP = 4
CAP = 24
LANES = 128
SUBLANES = 8


def packed_body(hidden_in, expert_ids, combine, w_gate, w_up, w_down):
    group_count = lax.axis_size("grp")
    loc_count = lax.axis_size("loc")
    slices = loc_count // EXP_GRP
    tok_count = hidden_in.shape[2]
    feature = hidden_in.shape[3]
    top_count = expert_ids.shape[3]
    token_rows = hidden_in.reshape(tok_count, feature)
    chosen = expert_ids.reshape(tok_count, top_count)
    weights = combine.reshape(tok_count, top_count).astype(jnp.float32)
    catalog = jnp.arange(group_count * EXP_GRP, dtype=jnp.int32)
    matches = (chosen[:, :, None] == catalog[None, None, :]).astype(jnp.float32)
    hit_table = jnp.sum(matches, axis=1)
    pick_table = jnp.einsum("tk,tke->te", weights, matches)
    hit_table = (
        hit_table.reshape(tok_count, group_count, EXP_GRP).transpose(1, 0, 2).astype(jnp.bfloat16)
    )
    pick_table = (
        pick_table.reshape(tok_count, group_count, EXP_GRP).transpose(1, 0, 2).astype(jnp.bfloat16)
    )
    arrivals_count = group_count * tok_count
    outgoing = token_rows[None, :, None, :] * hit_table[:, :, :, None]
    arrived, arr_hits, arr_picks = (
        lax.all_to_all(outgoing, "grp", split_axis=0, concat_axis=0, tiled=True),
        lax.all_to_all(hit_table, "grp", split_axis=0, concat_axis=0, tiled=True),
        lax.all_to_all(pick_table, "grp", split_axis=0, concat_axis=0, tiled=True),
    )
    arrived = arrived.reshape(arrivals_count, EXP_GRP, feature)
    flat_hits = arr_hits.reshape(arrivals_count, EXP_GRP).astype(jnp.float32)
    flat_picks = arr_picks.reshape(arrivals_count, EXP_GRP).astype(jnp.float32)
    slot_rank = jnp.cumsum(flat_hits, axis=0) - 1.0
    cell_index = jnp.arange(CAP, dtype=jnp.float32)
    selector = flat_hits.T[:, None, :] * (
        slot_rank.T[:, None, :] == cell_index[None, :, None]
    ).astype(jnp.float32)
    weighted = selector * flat_picks.T[:, None, :]
    compact_selector = selector.astype(jnp.bfloat16)
    packed = jnp.einsum(
        "jcm,mjd->jcd", compact_selector, arrived, preferred_element_type=jnp.float32
    ).astype(jnp.bfloat16)
    outbound = jnp.broadcast_to(packed[:, None, :, :], (EXP_GRP, slices, CAP, feature)).reshape(
        loc_count, CAP, feature
    )
    arrivals = lax.all_to_all(outbound, "loc", split_axis=0, concat_axis=0, tiled=True)
    item_count = arrivals.shape[1]
    flat_rows = arrivals.reshape(-1, feature)
    gate_out = jnp.dot(flat_rows, w_gate[0], preferred_element_type=jnp.float32)
    up_out = jnp.dot(flat_rows, w_up[0], preferred_element_type=jnp.float32)
    hidden_units = (jax.nn.silu(gate_out) * up_out).astype(jnp.bfloat16)
    result = jnp.dot(hidden_units, w_down[0], preferred_element_type=jnp.float32).astype(
        jnp.bfloat16
    )
    result = result.reshape(loc_count, item_count, feature)
    returned = lax.all_to_all(result, "loc", split_axis=0, concat_axis=0, tiled=True)
    slice_sum = jnp.sum(returned.reshape(EXP_GRP, slices, CAP, feature).astype(jnp.float32), axis=1)
    group_part = jnp.einsum(
        "jcm,jcd->md", weighted, slice_sum, precision=lax.Precision.HIGHEST
    ).astype(jnp.bfloat16)
    homeward = lax.all_to_all(
        group_part.reshape(group_count, tok_count, feature),
        "grp",
        split_axis=0,
        concat_axis=0,
        tiled=True,
    )
    summed = jnp.sum(homeward.astype(jnp.float32), axis=0)
    return summed.astype(jnp.bfloat16).reshape(1, 1, tok_count, feature)


def pairs(size, distance):
    return [(i, i ^ distance) for i in range(size)]


def swap(rows, axis, distance):
    return lax.ppermute(rows, axis, pairs(lax.axis_size(axis), distance))


def slide(rows, distance):
    count = lax.axis_size("loc")
    return lax.ppermute(rows, "loc", [(i, (i + distance) % count) for i in range(count)])


def turn(rows, steps):
    loc_count = lax.axis_size("loc")
    moves = [
        (g * loc_count + l, (g ^ steps[l % len(steps)]) * loc_count + l)
        for g in range(lax.axis_size("grp"))
        for l in range(loc_count)
    ]
    return lax.ppermute(rows, ("grp", "loc"), moves)


def tails_per_row(tok_count):
    return tok_count // (SUBLANES - tok_count)


def tail_width(tok_count, feature):
    return feature // (tails_per_row(tok_count) + 1)


def can_pack(tok_count, feature):
    spare = SUBLANES - tok_count
    if spare <= 0 or tok_count % spare:
        return False
    return feature % (LANES * (tails_per_row(tok_count) + 1)) == 0


def tail_places(tok_count, feature):
    per_row, width = tails_per_row(tok_count), tail_width(tok_count, feature)
    for t in range(tok_count):
        yield t, tok_count + t // per_row, (t % per_row) * width, width


def pack_rows(source, first, tok_count, feature, target):
    body = feature - tail_width(tok_count, feature)
    target[:tok_count, :body] = source[first : first + tok_count, :body]
    for t, row, lane, width in tail_places(tok_count, feature):
        target[row : row + 1, lane : lane + width] = source[first + t : first + t + 1, body:feature]


def unpack_rows(source, target, first, tok_count, feature):
    body = feature - tail_width(tok_count, feature)
    target[first : first + tok_count, :body] = source[:tok_count, :body]
    for t, row, lane, width in tail_places(tok_count, feature):
        target[first + t : first + t + 1, body:feature] = source[row : row + 1, lane : lane + width]


VMEM = pl.BlockSpec(memory_space=pltpu.VMEM)
HBM = pl.BlockSpec(memory_space=pltpu.HBM)


def in_hbm(array):
    return pltpu.with_memory_space_constraint(array, pltpu.HBM)


def call(kernel, outs, args, scratch=(), specs=None, flops=0, traffic=0):
    return pl.pallas_call(
        kernel,
        out_shape=outs,
        in_specs=specs or [VMEM] * len(args),
        out_specs=jax.tree.map(lambda _: VMEM, outs),
        scratch_shapes=list(scratch),
        compiler_params=pltpu.CompilerParams(vmem_limit_bytes=24 * 1024 * 1024),
        cost_estimate=pl.CostEstimate(flops=flops, bytes_accessed=traffic, transcendentals=0),
    )(*args)


def prepare_kernel(rows_hbm, ids_hbm, combine_hbm, out_ref, rows, ids, picks, wide, packed, sems):
    copies = [
        pltpu.make_async_copy(source, target, sems.at[i])
        for i, (source, target) in enumerate(
            ((rows_hbm, rows), (ids_hbm, ids), (combine_hbm, picks))
        )
    ]
    for c in copies:
        c.start()
    for c in copies:
        c.wait()
    tok_count, feature = rows.shape
    body = feature - tail_width(tok_count, feature)
    wide[...] = rows[...].astype(jnp.float32)
    packed[:, body:] = jnp.zeros((SUBLANES, LANES), jnp.float32)
    pack_rows(wide, 0, tok_count, feature, packed)
    weights = picks[...].astype(jnp.float32)
    lanes = lax.broadcasted_iota(jnp.int32, (1, LANES), 1)
    for t in range(tok_count):
        chosen = ids[t]
        row = jnp.zeros((1, LANES), jnp.float32)
        for k in range(chosen.shape[1]):
            row = row + jnp.where(lanes == chosen[:, k : k + 1], weights[t : t + 1, k : k + 1], 0.0)
        packed[t : t + 1, body:] = row
    out_ref[...] = packed[...].astype(jnp.bfloat16)


def join_kernel(*refs):
    pieces, out_ref = refs[:-1], refs[-1]
    whole = jnp.concatenate([piece[...].astype(jnp.float32) for piece in pieces], axis=0)
    out_ref[...] = whole.astype(jnp.bfloat16)


def fetch_kernel(gate_hbm, up_hbm, down_hbm, out_ref, sems):
    feature, units = gate_hbm.shape
    copies = [
        (gate_hbm, out_ref.at[:feature]),
        (up_hbm, out_ref.at[feature : 2 * feature]),
    ]
    for i in range(feature // LANES):
        lowest = 2 * feature + i * units
        copies.append(
            (down_hbm.at[:, i * LANES : (i + 1) * LANES], out_ref.at[lowest : lowest + units])
        )
    copies = [
        pltpu.make_async_copy(source, target, sems.at[i])
        for i, (source, target) in enumerate(copies)
    ]
    for c in copies:
        c.start()
    for c in copies:
        c.wait()


def expert_kernel(tok_count, slices, rows_ref, *refs):
    weights, (out_ref, packed, wide) = refs[:slices], refs[slices:]
    units = LANES
    feature = wide.shape[1] - LANES
    body = feature - tail_width(tok_count, feature)
    own_expert = lax.axis_index("grp") * EXP_GRP + lax.axis_index("loc") // slices
    packed[...] = rows_ref[...].astype(jnp.float32)
    for i in range(EXP_GRP):
        piece = packed.at[i * SUBLANES : (i + 1) * SUBLANES]
        unpack_rows(piece, wide, i * tok_count, tok_count, feature)
        wide[i * tok_count : (i + 1) * tok_count, feature:] = piece[:tok_count, body:]
    features = wide[:, :feature].astype(jnp.bfloat16)
    table = wide[:, feature:]
    lanes = lax.broadcasted_iota(jnp.int32, table.shape, 1)
    weight = jnp.sum(jnp.where(lanes == own_expert, table, 0.0), axis=1, keepdims=True)
    hidden, downs = [], []
    for w in weights:
        both = jnp.dot(
            features,
            jnp.concatenate([w[:feature], w[feature : 2 * feature]], axis=1),
            preferred_element_type=jnp.float32,
        )
        gate_out, up_out = both[:, :units], both[:, units:]
        hidden.append((gate_out / (1.0 + jnp.exp(-gate_out)) * up_out).astype(jnp.bfloat16))
        blocks = [
            w[2 * feature + i * units : 2 * feature + (i + 1) * units]
            for i in range(feature // LANES)
        ]
        downs.append(jnp.concatenate(blocks, axis=1))
    part = jnp.dot(
        jnp.concatenate(hidden, axis=1),
        jnp.concatenate(downs, axis=0),
        preferred_element_type=jnp.float32,
    )
    wide[:, :feature] = part * weight
    for i in range(EXP_GRP):
        piece = packed.at[i * SUBLANES : (i + 1) * SUBLANES]
        pack_rows(wide, i * tok_count, tok_count, feature, piece)
    out_ref[...] = packed[:, :body].astype(out_ref.dtype)


def combine_kernel(*refs):
    pieces, outs = refs[:EXP_GRP], refs[EXP_GRP:]
    total = pieces[0][...].astype(jnp.float32)
    for piece in pieces[1:]:
        total = total + piece[...].astype(jnp.float32)
    for i, out_ref in enumerate(outs):
        out_ref[...] = total[i * SUBLANES : (i + 1) * SUBLANES].astype(out_ref.dtype)


def finish_kernel(*refs):
    pieces, out_ref, packed, wide = refs[:-3], refs[-3], refs[-2], refs[-1]
    total = pieces[0][...].astype(jnp.float32)
    for piece in pieces[1:]:
        total = total + piece[...].astype(jnp.float32)
    packed[...] = total
    unpack_rows(packed, wide, 0, *wide.shape)
    out_ref[...] = wide[...].astype(out_ref.dtype)


def dense_body(hidden_in, expert_ids, combine, w_gate, w_up, w_down):
    slices = lax.axis_size("loc") // EXP_GRP
    tok_count = hidden_in.shape[2]
    feature = hidden_in.shape[3]
    top_count = expert_ids.shape[3]
    gathered = EXP_GRP * tok_count
    body = feature - tail_width(tok_count, feature)
    bf16, f32 = jnp.bfloat16, jnp.float32
    scratch = pltpu.VMEM

    blocks = (w_gate[0], w_up[0], w_down[0])
    own = call(
        prepare_kernel,
        jax.ShapeDtypeStruct((SUBLANES, body + LANES), bf16),
        (
            in_hbm(hidden_in.reshape(tok_count, feature)),
            in_hbm(expert_ids.reshape(tok_count, 1, top_count)),
            in_hbm(combine.reshape(tok_count, top_count)),
        ),
        [
            scratch((tok_count, feature), bf16),
            scratch((tok_count, 1, top_count), jnp.int32),
            scratch((tok_count, top_count), bf16),
            scratch((tok_count, feature), f32),
            scratch((SUBLANES, body + LANES), f32),
            pltpu.SemaphoreType.DMA((3,)),
        ],
        [HBM] * 3,
    )
    steps = range(1, EXP_GRP)
    pieces = [own] + [slide(own, slices * k) for k in steps]
    *blocks, pieces[0] = lax.optimization_barrier((*blocks, pieces[0]))
    size = sum(w.size for w in blocks)
    kept = call(
        fetch_kernel,
        jax.ShapeDtypeStruct((3 * feature, LANES), bf16),
        [in_hbm(w) for w in blocks],
        [pltpu.SemaphoreType.DMA((2 + feature // LANES,))],
        [HBM] * 3,
        traffic=2 * size,
    )
    kept, pieces = lax.optimization_barrier((kept, pieces))
    weights = [kept] + [swap(kept, "loc", k) for k in range(1, slices)]

    def run_expert(rows, dtype):
        return call(
            functools.partial(expert_kernel, tok_count, slices),
            jax.ShapeDtypeStruct((EXP_GRP * SUBLANES, body), dtype),
            (rows, *weights),
            [scratch(rows.shape, f32), scratch((gathered, feature + LANES), f32)],
            flops=2 * gathered * size * slices,
            traffic=2 * size * slices,
        )

    rows = call(
        join_kernel, jax.ShapeDtypeStruct((EXP_GRP * SUBLANES, body + LANES), bf16), pieces
    )
    first, second = [1 + i % 2 for i in range(slices)], [2 - i % 2 for i in range(slices)]
    beside, above = turn(rows, first), turn(rows, second)
    across = swap(rows, "grp", 3)
    returned = (
        turn(run_expert(beside, bf16), first),
        turn(run_expert(above, bf16), second),
        swap(run_expert(across, bf16), "grp", 3),
    )
    packed = (SUBLANES, body)
    sums = call(
        combine_kernel,
        [jax.ShapeDtypeStruct(packed, f32)] + [jax.ShapeDtypeStruct(packed, bf16)] * len(steps),
        (run_expert(rows, f32), *returned),
    )
    homeward = [slide(sums[k], -slices * k) for k in steps]
    total = call(
        finish_kernel,
        jax.ShapeDtypeStruct((tok_count, feature), bf16),
        (sums[0], *homeward),
        [scratch(packed, f32), scratch((tok_count, feature), f32)],
    )
    return total.reshape(1, 1, tok_count, feature)


def power_of_two(count):
    return count & (count - 1) == 0


def solution(mesh):
    group_count, loc_count = mesh.shape["grp"], mesh.shape["loc"]
    placed = (
        P("loc", "grp", None, None),
        P("loc", "grp", None, None),
        P("loc", "grp", None, None),
        P(("grp", "loc"), None, None),
        P(("grp", "loc"), None, None),
        P(("grp", "loc"), None, None),
    )
    dense_fits = group_count == EXP_GRP == 4 and power_of_two(loc_count)

    def layer(hidden_in, *others):
        tokens = hidden_in.shape[1] * hidden_in.shape[2]
        units = others[2].shape[2]
        small = tokens <= CAP and units == LANES and can_pack(*hidden_in.shape[2:])
        body = dense_body if dense_fits and small else packed_body
        return jax.shard_map(
            body, mesh=mesh, in_specs=placed, out_specs=P("loc", "grp", None, None), check_vma=False
        )(hidden_in, *others)

    return layer
```

```python
import functools

import jax
import jax.numpy as jnp
from jax import lax
from jax.experimental import pallas as pl
from jax.experimental.pallas import tpu as pltpu
from jax.sharding import PartitionSpec as P

EXP_GRP = 4
CAP = 24
LANES = 128
SUBLANES = 8


def packed_body(hidden_in, expert_ids, combine, w_gate, w_up, w_down):
    group_count = lax.axis_size("grp")
    loc_count = lax.axis_size("loc")
    slices = loc_count // EXP_GRP
    tok_count = hidden_in.shape[2]
    feature = hidden_in.shape[3]
    top_count = expert_ids.shape[3]
    token_rows = hidden_in.reshape(tok_count, feature)
    chosen = expert_ids.reshape(tok_count, top_count)
    weights = combine.reshape(tok_count, top_count).astype(jnp.float32)
    catalog = jnp.arange(group_count * EXP_GRP, dtype=jnp.int32)
    matches = (chosen[:, :, None] == catalog[None, None, :]).astype(jnp.float32)
    hit_table = jnp.sum(matches, axis=1)
    pick_table = jnp.einsum("tk,tke->te", weights, matches)
    hit_table = (
        hit_table.reshape(tok_count, group_count, EXP_GRP).transpose(1, 0, 2).astype(jnp.bfloat16)
    )
    pick_table = (
        pick_table.reshape(tok_count, group_count, EXP_GRP).transpose(1, 0, 2).astype(jnp.bfloat16)
    )
    arrivals_count = group_count * tok_count
    outgoing = token_rows[None, :, None, :] * hit_table[:, :, :, None]
    arrived, arr_hits, arr_picks = (
        lax.all_to_all(outgoing, "grp", split_axis=0, concat_axis=0, tiled=True),
        lax.all_to_all(hit_table, "grp", split_axis=0, concat_axis=0, tiled=True),
        lax.all_to_all(pick_table, "grp", split_axis=0, concat_axis=0, tiled=True),
    )
    arrived = arrived.reshape(arrivals_count, EXP_GRP, feature)
    flat_hits = arr_hits.reshape(arrivals_count, EXP_GRP).astype(jnp.float32)
    flat_picks = arr_picks.reshape(arrivals_count, EXP_GRP).astype(jnp.float32)
    slot_rank = jnp.cumsum(flat_hits, axis=0) - 1.0
    cell_index = jnp.arange(CAP, dtype=jnp.float32)
    selector = flat_hits.T[:, None, :] * (
        slot_rank.T[:, None, :] == cell_index[None, :, None]
    ).astype(jnp.float32)
    weighted = selector * flat_picks.T[:, None, :]
    compact_selector = selector.astype(jnp.bfloat16)
    packed = jnp.einsum(
        "jcm,mjd->jcd", compact_selector, arrived, preferred_element_type=jnp.float32
    ).astype(jnp.bfloat16)
    outbound = jnp.broadcast_to(packed[:, None, :, :], (EXP_GRP, slices, CAP, feature)).reshape(
        loc_count, CAP, feature
    )
    arrivals = lax.all_to_all(outbound, "loc", split_axis=0, concat_axis=0, tiled=True)
    item_count = arrivals.shape[1]
    flat_rows = arrivals.reshape(-1, feature)
    gate_out = jnp.dot(flat_rows, w_gate[0], preferred_element_type=jnp.float32)
    up_out = jnp.dot(flat_rows, w_up[0], preferred_element_type=jnp.float32)
    hidden_units = (jax.nn.silu(gate_out) * up_out).astype(jnp.bfloat16)
    result = jnp.dot(hidden_units, w_down[0], preferred_element_type=jnp.float32).astype(
        jnp.bfloat16
    )
    result = result.reshape(loc_count, item_count, feature)
    returned = lax.all_to_all(result, "loc", split_axis=0, concat_axis=0, tiled=True)
    slice_sum = jnp.sum(returned.reshape(EXP_GRP, slices, CAP, feature).astype(jnp.float32), axis=1)
    group_part = jnp.einsum(
        "jcm,jcd->md", weighted, slice_sum, precision=lax.Precision.HIGHEST
    ).astype(jnp.bfloat16)
    homeward = lax.all_to_all(
        group_part.reshape(group_count, tok_count, feature),
        "grp",
        split_axis=0,
        concat_axis=0,
        tiled=True,
    )
    summed = jnp.sum(homeward.astype(jnp.float32), axis=0)
    return summed.astype(jnp.bfloat16).reshape(1, 1, tok_count, feature)


def pairs(size, distance):
    return [(i, i ^ distance) for i in range(size)]


def swap(rows, axis, distance):
    return lax.ppermute(rows, axis, pairs(lax.axis_size(axis), distance))


def slide(rows, distance):
    count = lax.axis_size("loc")
    return lax.ppermute(rows, "loc", [(i, (i + distance) % count) for i in range(count)])


def turn(rows, steps):
    loc_count = lax.axis_size("loc")
    moves = [
        (g * loc_count + l, (g ^ steps[l % len(steps)]) * loc_count + l)
        for g in range(lax.axis_size("grp"))
        for l in range(loc_count)
    ]
    return lax.ppermute(rows, ("grp", "loc"), moves)


def tails_per_row(tok_count):
    return tok_count // (SUBLANES - tok_count)


def tail_width(tok_count, feature):
    return feature // (tails_per_row(tok_count) + 1)


def can_pack(tok_count, feature):
    spare = SUBLANES - tok_count
    if spare <= 0 or tok_count % spare:
        return False
    return feature % (LANES * (tails_per_row(tok_count) + 1)) == 0


def tail_places(tok_count, feature):
    per_row, width = tails_per_row(tok_count), tail_width(tok_count, feature)
    for t in range(tok_count):
        yield t, tok_count + t // per_row, (t % per_row) * width, width


def pack_rows(source, first, tok_count, feature, target):
    body = feature - tail_width(tok_count, feature)
    target[:tok_count, :body] = source[first : first + tok_count, :body]
    for t, row, lane, width in tail_places(tok_count, feature):
        target[row : row + 1, lane : lane + width] = source[first + t : first + t + 1, body:feature]


def unpack_rows(source, target, first, tok_count, feature):
    body = feature - tail_width(tok_count, feature)
    target[first : first + tok_count, :body] = source[:tok_count, :body]
    for t, row, lane, width in tail_places(tok_count, feature):
        target[first + t : first + t + 1, body:feature] = source[row : row + 1, lane : lane + width]


VMEM = pl.BlockSpec(memory_space=pltpu.VMEM)
HBM = pl.BlockSpec(memory_space=pltpu.HBM)


def in_hbm(array):
    return pltpu.with_memory_space_constraint(array, pltpu.HBM)


def call(kernel, outs, args, scratch=(), specs=None, flops=0, traffic=0):
    return pl.pallas_call(
        kernel,
        out_shape=outs,
        in_specs=specs or [VMEM] * len(args),
        out_specs=jax.tree.map(lambda _: VMEM, outs),
        scratch_shapes=list(scratch),
        compiler_params=pltpu.CompilerParams(vmem_limit_bytes=24 * 1024 * 1024),
        cost_estimate=pl.CostEstimate(flops=flops, bytes_accessed=traffic, transcendentals=0),
    )(*args)


def prepare_kernel(rows_hbm, ids_hbm, combine_hbm, out_ref, rows, ids, picks, wide, packed, sems):
    copies = [
        pltpu.make_async_copy(source, target, sems.at[i])
        for i, (source, target) in enumerate(
            ((rows_hbm, rows), (ids_hbm, ids), (combine_hbm, picks))
        )
    ]
    for c in copies:
        c.start()
    for c in copies:
        c.wait()
    tok_count, feature = rows.shape
    body = feature - tail_width(tok_count, feature)
    wide[...] = rows[...].astype(jnp.float32)
    packed[:, body:] = jnp.zeros((SUBLANES, LANES), jnp.float32)
    pack_rows(wide, 0, tok_count, feature, packed)
    weights = picks[...].astype(jnp.float32)
    chosen = jnp.concatenate([ids[t] for t in range(tok_count)], axis=0)
    lanes = lax.broadcasted_iota(jnp.int32, (tok_count, LANES), 1)
    table = jnp.zeros((tok_count, LANES), jnp.float32)
    for k in range(chosen.shape[1]):
        table = table + jnp.where(lanes == chosen[:, k : k + 1], weights[:, k : k + 1], 0.0)
    packed[:tok_count, body:] = table
    out_ref[...] = packed[...].astype(jnp.bfloat16)


def join_kernel(*refs):
    pieces, out_ref = refs[:-1], refs[-1]
    whole = jnp.concatenate([piece[...].astype(jnp.float32) for piece in pieces], axis=0)
    out_ref[...] = whole.astype(jnp.bfloat16)


def fetch_kernel(gate_hbm, up_hbm, down_hbm, out_ref, sems):
    feature, units = gate_hbm.shape
    copies = [
        (gate_hbm, out_ref.at[:feature]),
        (up_hbm, out_ref.at[feature : 2 * feature]),
    ]
    for i in range(feature // LANES):
        lowest = 2 * feature + i * units
        copies.append(
            (down_hbm.at[:, i * LANES : (i + 1) * LANES], out_ref.at[lowest : lowest + units])
        )
    copies = [
        pltpu.make_async_copy(source, target, sems.at[i])
        for i, (source, target) in enumerate(copies)
    ]
    for c in copies:
        c.start()
    for c in copies:
        c.wait()


def expert_kernel(tok_count, slices, rows_ref, *refs):
    weights, (out_ref, packed, wide) = refs[:slices], refs[slices:]
    units = LANES
    feature = wide.shape[1] - LANES
    body = feature - tail_width(tok_count, feature)
    own_expert = lax.axis_index("grp") * EXP_GRP + lax.axis_index("loc") // slices
    packed[...] = rows_ref[...].astype(jnp.float32)
    for i in range(EXP_GRP):
        piece = packed.at[i * SUBLANES : (i + 1) * SUBLANES]
        unpack_rows(piece, wide, i * tok_count, tok_count, feature)
        wide[i * tok_count : (i + 1) * tok_count, feature:] = piece[:tok_count, body:]
    features = wide[:, :feature].astype(jnp.bfloat16)
    table = wide[:, feature:]
    lanes = lax.broadcasted_iota(jnp.int32, table.shape, 1)
    weight = jnp.sum(jnp.where(lanes == own_expert, table, 0.0), axis=1, keepdims=True)
    hidden, downs = [], []
    for w in weights:
        both = jnp.dot(
            features,
            jnp.concatenate([w[:feature], w[feature : 2 * feature]], axis=1),
            preferred_element_type=jnp.float32,
        )
        gate_out, up_out = both[:, :units], both[:, units:]
        hidden.append((gate_out / (1.0 + jnp.exp(-gate_out)) * up_out).astype(jnp.bfloat16))
        blocks = [
            w[2 * feature + i * units : 2 * feature + (i + 1) * units]
            for i in range(feature // LANES)
        ]
        downs.append(jnp.concatenate(blocks, axis=1))
    part = jnp.dot(
        jnp.concatenate(hidden, axis=1),
        jnp.concatenate(downs, axis=0),
        preferred_element_type=jnp.float32,
    )
    wide[:, :feature] = part * weight
    for i in range(EXP_GRP):
        piece = packed.at[i * SUBLANES : (i + 1) * SUBLANES]
        pack_rows(wide, i * tok_count, tok_count, feature, piece)
    out_ref[...] = packed[:, :body].astype(out_ref.dtype)


def combine_kernel(*refs):
    pieces, outs = refs[:EXP_GRP], refs[EXP_GRP:]
    total = pieces[0][...].astype(jnp.float32)
    for piece in pieces[1:]:
        total = total + piece[...].astype(jnp.float32)
    for i, out_ref in enumerate(outs):
        out_ref[...] = total[i * SUBLANES : (i + 1) * SUBLANES].astype(out_ref.dtype)


def finish_kernel(*refs):
    pieces, out_ref, packed, wide = refs[:-3], refs[-3], refs[-2], refs[-1]
    total = pieces[0][...].astype(jnp.float32)
    for piece in pieces[1:]:
        total = total + piece[...].astype(jnp.float32)
    packed[...] = total
    unpack_rows(packed, wide, 0, *wide.shape)
    out_ref[...] = wide[...].astype(out_ref.dtype)


def dense_body(hidden_in, expert_ids, combine, w_gate, w_up, w_down):
    slices = lax.axis_size("loc") // EXP_GRP
    tok_count = hidden_in.shape[2]
    feature = hidden_in.shape[3]
    top_count = expert_ids.shape[3]
    gathered = EXP_GRP * tok_count
    body = feature - tail_width(tok_count, feature)
    bf16, f32 = jnp.bfloat16, jnp.float32
    scratch = pltpu.VMEM

    blocks = (w_gate[0], w_up[0], w_down[0])
    own = call(
        prepare_kernel,
        jax.ShapeDtypeStruct((SUBLANES, body + LANES), bf16),
        (
            in_hbm(hidden_in.reshape(tok_count, feature)),
            in_hbm(expert_ids.reshape(tok_count, 1, top_count)),
            in_hbm(combine.reshape(tok_count, top_count)),
        ),
        [
            scratch((tok_count, feature), bf16),
            scratch((tok_count, 1, top_count), jnp.int32),
            scratch((tok_count, top_count), bf16),
            scratch((tok_count, feature), f32),
            scratch((SUBLANES, body + LANES), f32),
            pltpu.SemaphoreType.DMA((3,)),
        ],
        [HBM] * 3,
    )
    steps = range(1, EXP_GRP)
    got = {k: slide(own, slices * k) for k in reversed(steps)}
    pieces = [own] + [got[k] for k in steps]
    *blocks, pieces[0] = lax.optimization_barrier((*blocks, pieces[0]))
    size = sum(w.size for w in blocks)
    kept = call(
        fetch_kernel,
        jax.ShapeDtypeStruct((3 * feature, LANES), bf16),
        [in_hbm(w) for w in blocks],
        [pltpu.SemaphoreType.DMA((2 + feature // LANES,))],
        [HBM] * 3,
        traffic=2 * size,
    )
    kept, pieces = lax.optimization_barrier((kept, pieces))
    weights = [kept] + [swap(kept, "loc", k) for k in range(1, slices)]

    def run_expert(rows, dtype):
        return call(
            functools.partial(expert_kernel, tok_count, slices),
            jax.ShapeDtypeStruct((EXP_GRP * SUBLANES, body), dtype),
            (rows, *weights),
            [scratch(rows.shape, f32), scratch((gathered, feature + LANES), f32)],
            flops=2 * gathered * size * slices,
            traffic=2 * size * slices,
        )

    rows = call(
        join_kernel, jax.ShapeDtypeStruct((EXP_GRP * SUBLANES, body + LANES), bf16), pieces
    )
    first, second = [1 + i % 2 for i in range(slices)], [2 - i % 2 for i in range(slices)]
    beside, above = turn(rows, first), turn(rows, second)
    across = swap(rows, "grp", 3)
    returned = (
        turn(run_expert(beside, bf16), first),
        turn(run_expert(above, bf16), second),
        swap(run_expert(across, bf16), "grp", 3),
    )
    packed = (SUBLANES, body)
    sums = call(
        combine_kernel,
        [jax.ShapeDtypeStruct(packed, f32)] + [jax.ShapeDtypeStruct(packed, bf16)] * len(steps),
        (run_expert(rows, f32), *returned),
    )
    homeward = [slide(sums[k], -slices * k) for k in reversed(steps)]
    total = call(
        finish_kernel,
        jax.ShapeDtypeStruct((tok_count, feature), bf16),
        (sums[0], *homeward),
        [scratch(packed, f32), scratch((tok_count, feature), f32)],
    )
    return total.reshape(1, 1, tok_count, feature)


def power_of_two(count):
    return count & (count - 1) == 0


def solution(mesh):
    group_count, loc_count = mesh.shape["grp"], mesh.shape["loc"]
    placed = (
        P("loc", "grp", None, None),
        P("loc", "grp", None, None),
        P("loc", "grp", None, None),
        P(("grp", "loc"), None, None),
        P(("grp", "loc"), None, None),
        P(("grp", "loc"), None, None),
    )
    dense_fits = group_count == EXP_GRP == 4 and power_of_two(loc_count)

    def layer(hidden_in, *others):
        tokens = hidden_in.shape[1] * hidden_in.shape[2]
        units = others[2].shape[2]
        small = tokens <= CAP and units == LANES and can_pack(*hidden_in.shape[2:])
        body = dense_body if dense_fits and small else packed_body
        return jax.shard_map(
            body, mesh=mesh, in_specs=placed, out_specs=P("loc", "grp", None, None), check_vma=False
        )(hidden_in, *others)

    return layer
```

```python
import functools

import jax
import jax.numpy as jnp
from jax import lax
from jax.experimental import pallas as pl
from jax.experimental.pallas import tpu as pltpu
from jax.sharding import PartitionSpec as P

EXP_GRP = 4
CAP = 24
LANES = 128
SUBLANES = 8


def packed_body(hidden_in, expert_ids, combine, w_gate, w_up, w_down):
    group_count = lax.axis_size("grp")
    loc_count = lax.axis_size("loc")
    slices = loc_count // EXP_GRP
    tok_count = hidden_in.shape[2]
    feature = hidden_in.shape[3]
    top_count = expert_ids.shape[3]
    token_rows = hidden_in.reshape(tok_count, feature)
    chosen = expert_ids.reshape(tok_count, top_count)
    weights = combine.reshape(tok_count, top_count).astype(jnp.float32)
    catalog = jnp.arange(group_count * EXP_GRP, dtype=jnp.int32)
    matches = (chosen[:, :, None] == catalog[None, None, :]).astype(jnp.float32)
    hit_table = jnp.sum(matches, axis=1)
    pick_table = jnp.einsum("tk,tke->te", weights, matches)
    hit_table = (
        hit_table.reshape(tok_count, group_count, EXP_GRP).transpose(1, 0, 2).astype(jnp.bfloat16)
    )
    pick_table = (
        pick_table.reshape(tok_count, group_count, EXP_GRP).transpose(1, 0, 2).astype(jnp.bfloat16)
    )
    arrivals_count = group_count * tok_count
    outgoing = token_rows[None, :, None, :] * hit_table[:, :, :, None]
    arrived, arr_hits, arr_picks = (
        lax.all_to_all(outgoing, "grp", split_axis=0, concat_axis=0, tiled=True),
        lax.all_to_all(hit_table, "grp", split_axis=0, concat_axis=0, tiled=True),
        lax.all_to_all(pick_table, "grp", split_axis=0, concat_axis=0, tiled=True),
    )
    arrived = arrived.reshape(arrivals_count, EXP_GRP, feature)
    flat_hits = arr_hits.reshape(arrivals_count, EXP_GRP).astype(jnp.float32)
    flat_picks = arr_picks.reshape(arrivals_count, EXP_GRP).astype(jnp.float32)
    slot_rank = jnp.cumsum(flat_hits, axis=0) - 1.0
    cell_index = jnp.arange(CAP, dtype=jnp.float32)
    selector = flat_hits.T[:, None, :] * (
        slot_rank.T[:, None, :] == cell_index[None, :, None]
    ).astype(jnp.float32)
    weighted = selector * flat_picks.T[:, None, :]
    compact_selector = selector.astype(jnp.bfloat16)
    packed = jnp.einsum(
        "jcm,mjd->jcd", compact_selector, arrived, preferred_element_type=jnp.float32
    ).astype(jnp.bfloat16)
    outbound = jnp.broadcast_to(packed[:, None, :, :], (EXP_GRP, slices, CAP, feature)).reshape(
        loc_count, CAP, feature
    )
    arrivals = lax.all_to_all(outbound, "loc", split_axis=0, concat_axis=0, tiled=True)
    item_count = arrivals.shape[1]
    flat_rows = arrivals.reshape(-1, feature)
    gate_out = jnp.dot(flat_rows, w_gate[0], preferred_element_type=jnp.float32)
    up_out = jnp.dot(flat_rows, w_up[0], preferred_element_type=jnp.float32)
    hidden_units = (jax.nn.silu(gate_out) * up_out).astype(jnp.bfloat16)
    result = jnp.dot(hidden_units, w_down[0], preferred_element_type=jnp.float32).astype(
        jnp.bfloat16
    )
    result = result.reshape(loc_count, item_count, feature)
    returned = lax.all_to_all(result, "loc", split_axis=0, concat_axis=0, tiled=True)
    slice_sum = jnp.sum(returned.reshape(EXP_GRP, slices, CAP, feature).astype(jnp.float32), axis=1)
    group_part = jnp.einsum(
        "jcm,jcd->md", weighted, slice_sum, precision=lax.Precision.HIGHEST
    ).astype(jnp.bfloat16)
    homeward = lax.all_to_all(
        group_part.reshape(group_count, tok_count, feature),
        "grp",
        split_axis=0,
        concat_axis=0,
        tiled=True,
    )
    summed = jnp.sum(homeward.astype(jnp.float32), axis=0)
    return summed.astype(jnp.bfloat16).reshape(1, 1, tok_count, feature)


def pairs(size, distance):
    return [(i, i ^ distance) for i in range(size)]


def swap(rows, axis, distance):
    return lax.ppermute(rows, axis, pairs(lax.axis_size(axis), distance))


def slide(rows, distance):
    count = lax.axis_size("loc")
    return lax.ppermute(rows, "loc", [(i, (i - distance) % count) for i in range(count)])


def turn(rows, steps):
    loc_count = lax.axis_size("loc")
    moves = [
        (g * loc_count + l, (g ^ steps[l % len(steps)]) * loc_count + l)
        for g in range(lax.axis_size("grp"))
        for l in range(loc_count)
    ]
    return lax.ppermute(rows, ("grp", "loc"), moves)


def tails_per_row(tok_count):
    return tok_count // (SUBLANES - tok_count)


def tail_width(tok_count, feature):
    return feature // (tails_per_row(tok_count) + 1)


def can_pack(tok_count, feature):
    spare = SUBLANES - tok_count
    if spare <= 0 or tok_count % spare:
        return False
    return feature % (LANES * (tails_per_row(tok_count) + 1)) == 0


def tail_places(tok_count, feature):
    per_row, width = tails_per_row(tok_count), tail_width(tok_count, feature)
    for t in range(tok_count):
        yield t, tok_count + t // per_row, (t % per_row) * width, width


def pack_rows(source, first, tok_count, feature, target):
    body = feature - tail_width(tok_count, feature)
    target[:tok_count, :body] = source[first : first + tok_count, :body]
    for t, row, lane, width in tail_places(tok_count, feature):
        target[row : row + 1, lane : lane + width] = source[first + t : first + t + 1, body:feature]


def unpack_rows(source, target, first, tok_count, feature):
    body = feature - tail_width(tok_count, feature)
    target[first : first + tok_count, :body] = source[:tok_count, :body]
    for t, row, lane, width in tail_places(tok_count, feature):
        target[first + t : first + t + 1, body:feature] = source[row : row + 1, lane : lane + width]


VMEM = pl.BlockSpec(memory_space=pltpu.VMEM)
HBM = pl.BlockSpec(memory_space=pltpu.HBM)


def in_hbm(array):
    return pltpu.with_memory_space_constraint(array, pltpu.HBM)


def call(kernel, outs, args, scratch=(), specs=None, flops=0, traffic=0):
    return pl.pallas_call(
        kernel,
        out_shape=outs,
        in_specs=specs or [VMEM] * len(args),
        out_specs=jax.tree.map(lambda _: VMEM, outs),
        scratch_shapes=list(scratch),
        compiler_params=pltpu.CompilerParams(vmem_limit_bytes=24 * 1024 * 1024),
        cost_estimate=pl.CostEstimate(flops=flops, bytes_accessed=traffic, transcendentals=0),
    )(*args)


def prepare_kernel(rows_hbm, ids_hbm, combine_hbm, out_ref, rows, ids, picks, wide, packed, sems):
    copies = [
        pltpu.make_async_copy(source, target, sems.at[i])
        for i, (source, target) in enumerate(
            ((rows_hbm, rows), (ids_hbm, ids), (combine_hbm, picks))
        )
    ]
    for c in copies:
        c.start()
    for c in copies:
        c.wait()
    tok_count, feature = rows.shape
    body = feature - tail_width(tok_count, feature)
    wide[...] = rows[...].astype(jnp.float32)
    packed[:, body:] = jnp.zeros((SUBLANES, LANES), jnp.float32)
    pack_rows(wide, 0, tok_count, feature, packed)
    weights = picks[...].astype(jnp.float32)
    chosen = jnp.concatenate([ids[t] for t in range(tok_count)], axis=0)
    lanes = lax.broadcasted_iota(jnp.int32, (tok_count, LANES), 1)
    table = jnp.zeros((tok_count, LANES), jnp.float32)
    for k in range(chosen.shape[1]):
        table = table + jnp.where(lanes == chosen[:, k : k + 1], weights[:, k : k + 1], 0.0)
    packed[:tok_count, body:] = table
    out_ref[...] = packed[...].astype(jnp.bfloat16)


def join_kernel(*refs):
    pieces, out_ref = refs[:-1], refs[-1]
    whole = jnp.concatenate([piece[...].astype(jnp.float32) for piece in pieces], axis=0)
    out_ref[...] = whole.astype(jnp.bfloat16)


def fetch_kernel(gate_hbm, up_hbm, down_hbm, out_ref, sems):
    feature, units = gate_hbm.shape
    copies = [
        (gate_hbm, out_ref.at[:feature]),
        (up_hbm, out_ref.at[feature : 2 * feature]),
    ]
    for i in range(feature // LANES):
        lowest = 2 * feature + i * units
        copies.append(
            (down_hbm.at[:, i * LANES : (i + 1) * LANES], out_ref.at[lowest : lowest + units])
        )
    copies = [
        pltpu.make_async_copy(source, target, sems.at[i])
        for i, (source, target) in enumerate(copies)
    ]
    for c in copies:
        c.start()
    for c in copies:
        c.wait()


def expert_kernel(tok_count, slices, rows_ref, *refs):
    weights, (out_ref, packed, wide) = refs[:slices], refs[slices:]
    units = LANES
    feature = wide.shape[1] - LANES
    body = feature - tail_width(tok_count, feature)
    own_expert = lax.axis_index("grp") * EXP_GRP + lax.axis_index("loc") // slices
    packed[...] = rows_ref[...].astype(jnp.float32)
    for i in range(EXP_GRP):
        piece = packed.at[i * SUBLANES : (i + 1) * SUBLANES]
        unpack_rows(piece, wide, i * tok_count, tok_count, feature)
        wide[i * tok_count : (i + 1) * tok_count, feature:] = piece[:tok_count, body:]
    features = wide[:, :feature].astype(jnp.bfloat16)
    table = wide[:, feature:]
    lanes = lax.broadcasted_iota(jnp.int32, table.shape, 1)
    weight = jnp.sum(jnp.where(lanes == own_expert, table, 0.0), axis=1, keepdims=True)
    hidden, downs = [], []
    for w in weights:
        both = jnp.dot(
            features,
            jnp.concatenate([w[:feature], w[feature : 2 * feature]], axis=1),
            preferred_element_type=jnp.float32,
        )
        gate_out, up_out = both[:, :units], both[:, units:]
        hidden.append((gate_out / (1.0 + jnp.exp(-gate_out)) * up_out).astype(jnp.bfloat16))
        blocks = [
            w[2 * feature + i * units : 2 * feature + (i + 1) * units]
            for i in range(feature // LANES)
        ]
        downs.append(jnp.concatenate(blocks, axis=1))
    part = jnp.dot(
        jnp.concatenate(hidden, axis=1),
        jnp.concatenate(downs, axis=0),
        preferred_element_type=jnp.float32,
    )
    wide[:, :feature] = part * weight
    for i in range(EXP_GRP):
        piece = packed.at[i * SUBLANES : (i + 1) * SUBLANES]
        pack_rows(wide, i * tok_count, tok_count, feature, piece)
    out_ref[...] = packed[:, :body].astype(out_ref.dtype)


def combine_kernel(slices, *refs):
    pieces, outs, total = refs[:EXP_GRP], refs[EXP_GRP:-1], refs[-1]
    summed = pieces[0][...].astype(jnp.float32)
    for piece in pieces[1:]:
        summed = summed + piece[...].astype(jnp.float32)
    total[...] = summed
    member = lax.axis_index("loc") // slices
    for k, out_ref in enumerate(outs):
        slot = member ^ ((member + EXP_GRP - k) % EXP_GRP)
        lowest = pl.multiple_of(slot * SUBLANES, SUBLANES)
        out_ref[...] = total[pl.ds(lowest, SUBLANES), :].astype(out_ref.dtype)


def finish_kernel(*refs):
    pieces, out_ref, packed, wide = refs[:-3], refs[-3], refs[-2], refs[-1]
    total = pieces[0][...].astype(jnp.float32)
    for piece in pieces[1:]:
        total = total + piece[...].astype(jnp.float32)
    packed[...] = total
    unpack_rows(packed, wide, 0, *wide.shape)
    out_ref[...] = wide[...].astype(out_ref.dtype)


def dense_body(hidden_in, expert_ids, combine, w_gate, w_up, w_down):
    slices = lax.axis_size("loc") // EXP_GRP
    tok_count = hidden_in.shape[2]
    feature = hidden_in.shape[3]
    top_count = expert_ids.shape[3]
    gathered = EXP_GRP * tok_count
    body = feature - tail_width(tok_count, feature)
    bf16, f32 = jnp.bfloat16, jnp.float32
    scratch = pltpu.VMEM

    blocks = (w_gate[0], w_up[0], w_down[0])
    own = call(
        prepare_kernel,
        jax.ShapeDtypeStruct((SUBLANES, body + LANES), bf16),
        (
            in_hbm(hidden_in.reshape(tok_count, feature)),
            in_hbm(expert_ids.reshape(tok_count, 1, top_count)),
            in_hbm(combine.reshape(tok_count, top_count)),
        ),
        [
            scratch((tok_count, feature), bf16),
            scratch((tok_count, 1, top_count), jnp.int32),
            scratch((tok_count, top_count), bf16),
            scratch((tok_count, feature), f32),
            scratch((SUBLANES, body + LANES), f32),
            pltpu.SemaphoreType.DMA((3,)),
        ],
        [HBM] * 3,
    )
    steps = range(1, EXP_GRP)
    got = {k: swap(own, "loc", slices * k) for k in reversed(steps)}
    pieces = [own] + [got[k] for k in steps]
    *blocks, pieces[0] = lax.optimization_barrier((*blocks, pieces[0]))
    size = sum(w.size for w in blocks)
    kept = call(
        fetch_kernel,
        jax.ShapeDtypeStruct((3 * feature, LANES), bf16),
        [in_hbm(w) for w in blocks],
        [pltpu.SemaphoreType.DMA((2 + feature // LANES,))],
        [HBM] * 3,
        traffic=2 * size,
    )
    kept, pieces = lax.optimization_barrier((kept, pieces))
    weights = [kept] + [swap(kept, "loc", k) for k in range(1, slices)]

    def run_expert(rows, dtype):
        return call(
            functools.partial(expert_kernel, tok_count, slices),
            jax.ShapeDtypeStruct((EXP_GRP * SUBLANES, body), dtype),
            (rows, *weights),
            [scratch(rows.shape, f32), scratch((gathered, feature + LANES), f32)],
            flops=2 * gathered * size * slices,
            traffic=2 * size * slices,
        )

    rows = call(
        join_kernel, jax.ShapeDtypeStruct((EXP_GRP * SUBLANES, body + LANES), bf16), pieces
    )
    first, second = [1 + i % 2 for i in range(slices)], [2 - i % 2 for i in range(slices)]
    beside, above = turn(rows, first), turn(rows, second)
    across = swap(rows, "grp", 3)
    returned = (
        turn(run_expert(beside, bf16), first),
        turn(run_expert(above, bf16), second),
        swap(run_expert(across, bf16), "grp", 3),
    )
    packed = (SUBLANES, body)
    sums = call(
        functools.partial(combine_kernel, slices),
        [jax.ShapeDtypeStruct(packed, f32)] + [jax.ShapeDtypeStruct(packed, bf16)] * len(steps),
        (run_expert(rows, f32), *returned),
        [scratch((EXP_GRP * SUBLANES, body), f32)],
    )
    homeward = [slide(sums[k], slices * k) for k in reversed(steps)]
    total = call(
        finish_kernel,
        jax.ShapeDtypeStruct((tok_count, feature), bf16),
        (sums[0], *homeward),
        [scratch(packed, f32), scratch((tok_count, feature), f32)],
    )
    return total.reshape(1, 1, tok_count, feature)


def power_of_two(count):
    return count & (count - 1) == 0


def solution(mesh):
    group_count, loc_count = mesh.shape["grp"], mesh.shape["loc"]
    placed = (
        P("loc", "grp", None, None),
        P("loc", "grp", None, None),
        P("loc", "grp", None, None),
        P(("grp", "loc"), None, None),
        P(("grp", "loc"), None, None),
        P(("grp", "loc"), None, None),
    )
    dense_fits = group_count == EXP_GRP == 4 and power_of_two(loc_count)

    def layer(hidden_in, *others):
        tokens = hidden_in.shape[1] * hidden_in.shape[2]
        units = others[2].shape[2]
        small = tokens <= CAP and units == LANES and can_pack(*hidden_in.shape[2:])
        body = dense_body if dense_fits and small else packed_body
        return jax.shard_map(
            body, mesh=mesh, in_specs=placed, out_specs=P("loc", "grp", None, None), check_vma=False
        )(hidden_in, *others)

    return layer
```
